128 devices in a mesh: pair: 32 (over x, y, core), red: 4 (over z).
Axes of the slice: x: 4, y: 4, z: 4, core: 2. Of those that a mesh axis runs over, the one named last changes fastest.
Arguments:
- amplitudes: float32 [1024, 16, 9216], P('pair', None, 'red'), may hold values from -6 to 6
- tile_occ: int32 [1024], P('pair'), may hold values from 0 to 3
- tile_virt: int32 [1024, 1], P('pair'), may hold values from 0 to 31; in each aligned block of 32 rows (0 to 31, 32 to 63, ...) at most 2 rows name the same one
- owner: int32 [32], replicated, may hold values from 0 to 31, each once
- integrals: float32 [32, 9216, 1536], P('pair', 'red'), may hold values from -0.0625 to 0.0625
Outputs:
- residual: float32 [128, 16, 1536], P('pair', None, 'red')
The draws below stay inside these ranges and needn't reach their ends.
Inputs may be any that keep to these rules, and one draw needn't show every extreme that they name: `tile_virt`: among the 32 tiles of one device, no virtual-pair tile is named more than 2 times, and in every draw some is named exactly 2 times. `owner`: each index of pair holds exactly one virtual-pair tile's integrals.
All inputs are finite; a program needn't handle non-finite values.
Results may differ from the reference program's by a relative error of at most 0.0001.
Values sent between devices are 32-bit elements; how exact they have to be, the bound alone decides.
A program may use at most 128 MiB of HBM per device.

```python
import math
import jax
import jax.numpy as jnp
import numpy as np
from jax import lax

TILE = 9216
AW = 1536
OROWS = 16
OBLK = 4
CAP = 2
NCT = 32
SLOTS = 32
N_PAIR = 32


def plant(array, rng, least, top_value):
    longest = array.shape.index(max(array.shape))
    spots = []
    for shift in (0, 1):
        where = [jax.random.randint(jax.random.fold_in(rng, axis), (), 0, length) for axis, length in enumerate(array.shape)]
        where[longest] = (where[longest] + shift) % array.shape[longest]
        spots.append(tuple(where))
    return array.at[spots[0]].set(least).at[spots[1]].set(top_value)


def steps_of(own_key, shape, shards, low, top_value):
    level, own = 1.0, jax.random.fold_in(own_key, 6)
    for position, blocks in shards:
        heights = jnp.exp(jax.random.uniform(jax.random.fold_in(own, position), (blocks,), jnp.float32, low / len(shards), top_value / len(shards)))
        level = level * jnp.repeat(heights, shape[position] // blocks).reshape([-1 if axis == position else 1 for axis in range(len(shape))])
    return level


def assign_block(rng, own, number, rows, count, top, most, lean):
    sequence = jax.random.permutation(rng, count)
    heavy_load, common = shares(count, rows * top, most, lean, True), shares(count, rows * top, most, lean, False)
    places = jnp.arange(count)

    def named(tallies, rotation):
        used = int((tallies > 0).sum())
        fixed = max(1, used // 4)
        moved = fixed + (places - fixed + rotation * (used - fixed)) % max(1, count - fixed)
        return jnp.zeros((count,), jnp.int32).at[sequence[jnp.where(places < fixed, places, moved)]].set(jnp.asarray(tallies, jnp.int32))

    tallies = jnp.where(number % 4 == 0, named(heavy_load, number // 4), named(common, number - number // 4 - 1))
    mixed = jax.random.permutation(jax.random.fold_in(own, 3), count)
    donor, receiver = mixed[0:count // 2 * 2:2], mixed[1:count // 2 * 2:2]
    slack = jnp.minimum(tallies[donor] - 1, most - tallies[receiver]) // 2
    slack = jnp.where((donor == sequence[0]) | (receiver == sequence[0]) | (tallies[receiver] == 0), 0, jnp.maximum(slack, 0))
    moved = jax.random.randint(jax.random.fold_in(own, 4), (count // 2,), 0, 1 << 20) % (slack + 1)
    tallies = tallies.at[donor].add(-moved).at[receiver].add(moved)
    members = jnp.searchsorted(jnp.cumsum(tallies), jnp.arange(rows * top), side="right").astype(jnp.int32)
    table = members.reshape(top, rows).T
    table = table[jax.random.permutation(jax.random.fold_in(own, 1), rows)]
    rotation = jax.random.randint(jax.random.fold_in(own, 2), (rows, 1), 0, top)
    return jnp.take_along_axis(table, (jnp.arange(top)[None, :] + rotation) % top, axis=1)


def shares(amount, total, most, skew, full):
    loads = [(1 << 20) // math.isqrt(rank ** skew) + 1 for rank in range(1, amount + 1)]
    largest = most if full else min(most, max(-(-total // amount), total * loads[0] // sum(loads)))
    least = 1 if total - largest >= amount - 1 else 0
    given, spare = [largest] + [least] * (amount - 1), total - largest - least * (amount - 1)
    while spare > 0:
        candidates = [i for i in range(1, amount) if given[i] < largest] or [i for i in range(1, amount) if given[i] < most]
        pool, left = sum([loads[i] for i in candidates]), spare
        for i in candidates:
            more = min(most - given[i], max(1, left * loads[i] // pool), spare)
            given[i] = given[i] + more
            spare = spare - more
    return np.array(given)


def noise(own_key, shape, width, limit, split=(), kind=jnp.bfloat16):
    array = jax.random.normal(own_key, shape, jnp.float32) * width
    if len(split) > 0:
        array = steps_of(own_key, shape, split, -0.22, 0.18) * array
    return jnp.clip(array, min=-limit, max=limit).astype(kind)


def setup_inputs(seed: int = 0) -> dict:
    arg_keys = jax.random.split(jax.random.key(seed), 6)
    amplitudes = noise(arg_keys[0], (N_PAIR * SLOTS, OROWS, TILE), 1.0, 6.0, ((0, 32), (2, 4)), jnp.float32)
    tile_occ = plant(jax.random.randint(arg_keys[1], (N_PAIR * SLOTS,), 0, OBLK), jax.random.fold_in(arg_keys[1], 1), 0, OBLK - 1).astype(jnp.int32)
    tile_virt_keys = jax.random.split(jax.random.fold_in(arg_keys[2], 1), (N_PAIR * SLOTS) // SLOTS)
    tile_virt_turns = jax.random.permutation(jax.random.fold_in(arg_keys[2], 3), (N_PAIR * SLOTS) // SLOTS)
    tile_virt = jax.vmap(lambda own, number: assign_block(jax.random.fold_in(arg_keys[2], 2), own, number, SLOTS, NCT, 1, CAP, 2))(tile_virt_keys, tile_virt_turns).reshape((N_PAIR * SLOTS, 1))
    owner = jax.random.permutation(arg_keys[3], NCT).astype(jnp.int32)
    integrals = noise(arg_keys[4], (N_PAIR, TILE, AW), TILE ** -0.5, 0.0625, ((0, 32), (1, 4)), jnp.float32)
    return dict(amplitudes=amplitudes, tile_occ=tile_occ, tile_virt=tile_virt, owner=owner, integrals=integrals)


def reference(amplitudes, tile_occ, tile_virt, owner, integrals):
    count = N_PAIR * SLOTS
    device_of = jnp.arange(count, dtype=jnp.int32) // SLOTS
    target = (device_of * OBLK + tile_occ).astype(jnp.int32)
    holder = owner[tile_virt[:, 0]].astype(jnp.int32)

    def add_tile(total, item):
        amp, row, who = item
        block = lax.dynamic_index_in_dim(integrals, who, 0, keepdims=False)
        product = jnp.dot(amp, block, precision=lax.Precision.HIGHEST, preferred_element_type=jnp.float32)
        return total.at[row].add(product), None

    start = jnp.zeros((N_PAIR * OBLK, OROWS, AW), jnp.float32)
    total, unused = lax.scan(add_tile, start, (amplitudes, target, holder))
    return total
```

```python
import functools

import jax
import jax.numpy as jnp
from jax import lax
from jax.experimental import pallas as pl
from jax.experimental.pallas import tpu as pltpu
from jax.sharding import PartitionSpec as P

MESH = pl.DeviceIdType.MESH
OBLK = 4
ROWS = 16
KDIM = 2304
NCOL = 1536
ZCOL = 384
NONE = 1 << 20

OFFSETS = (
    (0, 0), (1, 0),
    (0, 1), (3, 0),
    (0, 3), (1, 1),
    (3, 3), (1, 3),
    (3, 1), (2, 0),
    (0, 2), (2, 2),
    (2, 1), (2, 3),
    (1, 2), (3, 2),
)
GROUPS = 8
RELAYED = 12
RELAY_VIA = ((2, 0), (2, 0), (0, 2), (0, 2))
RELAY_ON = ((0, 1), (0, 3), (1, 0), (3, 0))
WINDOW = 3


def kernel(code0, code1, holds, amp_hbm, int_hbm, out_ref,
           amp, packed, relay, got, bhi, blo, stage, lhs, prod, zgot, summed, back,
           amp_sem, stage_sem, send_sem, got_sem, relay_send, relay_sem, forward_send,
           z_send, z_sem, back_send, back_sem):
    me = lax.axis_index("pair")
    z = lax.axis_index("red")
    x, y, c = me // 8, (me // 2) % 4, me % 2

    def chip(off, sign=1):
        dx, dy = off
        if sign < 0:
            dx, dy = 4 - dx, 4 - dy
        return lax.rem(x + dx, 4) * 4 + lax.rem(y + dy, 4)

    def remote(src, dst, ssem, rsem, pair, layer):
        return pltpu.make_async_remote_copy(
            src_ref=src, dst_ref=dst, send_sem=ssem, recv_sem=rsem,
            device_id=(pair, layer), device_id_type=MESH)

    barrier = pltpu.get_barrier_semaphore()

    def greet(i, carry):
        pl.semaphore_signal(barrier, inc=1, device_id=(lax.rem(me + i, 32), z), device_id_type=MESH)
        return carry

    lax.fori_loop(1, 32, greet, 0)
    for i in range(1, 4):
        pl.semaphore_signal(barrier, inc=1, device_id=(me, lax.rem(z + i, 4)), device_id_type=MESH)

    amp_copy = pltpu.make_async_copy(amp_hbm, amp, amp_sem)
    amp_copy.start()

    def load_stage(i):
        return pltpu.make_async_copy(int_hbm.at[0, pl.ds(i * 256, 256), :], stage.at[i % 2], stage_sem.at[i % 2])

    load_stage(0).start()
    load_stage(1).start()
    amp_copy.wait()

    def codes(k, oc):
        v = holds[chip(OFFSETS[k]) * 2 + oc]
        return code0[v], code1[v]

    def pack(k):
        for oc in range(2):
            first, second = codes(k, oc)
            one = jnp.where(first < NONE, first, 0) // OBLK
            two = jnp.where(second > first, second, 0) // OBLK
            packed[k, oc, 0:ROWS, :] = amp[one]
            packed[k, oc, ROWS:2 * ROWS, :] = amp[two]

    def send(k):
        if k >= RELAYED:
            r = k - RELAYED
            remote(packed.at[k], relay.at[r], relay_send.at[r], relay_sem.at[r],
                   chip(RELAY_VIA[r]) * 2 + c, z).start()
        elif k == 0:
            remote(packed.at[0, 1 - c], got.at[0, c], send_sem.at[0, 0], got_sem.at[0, c], me + 1 - 2 * c, z).start()
            pltpu.make_async_copy(packed.at[0, c], got.at[0, c], got_sem.at[0, c]).start()
        else:
            for oc in range(2):
                remote(packed.at[k, oc], got.at[k, c], send_sem.at[k, oc], got_sem.at[k, c],
                       chip(OFFSETS[k]) * 2 + oc, z).start()

    def forward(r):
        remote(packed.at[0], relay.at[r], relay_send.at[r], relay_sem.at[r], me + 1 - 2 * c, z).wait_recv()
        for oc in range(2):
            remote(relay.at[r, oc], got.at[RELAYED + r, c], forward_send.at[r, oc], got_sem.at[RELAYED + r, c],
                   chip(RELAY_ON[r]) * 2 + oc, z).start()

    first = [0, 1, 2, 3, 12, 13, 14, 15, 4, 5]
    for k in first[:4]:
        pack(k)
    pl.semaphore_wait(barrier, 34)
    for k in first[:4]:
        send(k)
    for k in first[4:]:
        pack(k)
        send(k)

    def split(i):
        load_stage(i).wait()
        block = stage.at[i % 2]

        def rows(t, carry):
            at = pl.multiple_of(t * 16, 16)
            for q in range(4):
                part = block[pl.ds(at, 16), q * ZCOL:(q + 1) * ZCOL]
                high = part.astype(jnp.bfloat16)
                to = pl.ds(pl.multiple_of(i * 256 + at, 16), 16)
                bhi[q, to, :] = high
                blo[q, to, :] = (part - high.astype(jnp.float32)).astype(jnp.bfloat16)
            return carry

        lax.fori_loop(0, 16, rows, 0)

    for i in range(9):
        split(i)
        if i + 2 < 9:
            load_stage(i + 2).start()

    def give_back(j):
        for i in range(3):
            remote(prod.at[j, i], zgot.at[j, i], z_send.at[j, i], z_sem.at[j, i], me, lax.rem(z + 1, 4)).wait_recv()

        def rows(t, carry):
            at = pl.ds(pl.multiple_of(t * 16, 16), 16)
            summed[j, at, :] = (prod[j, 3, at, :] + zgot[j, 0, at, :]) + (zgot[j, 1, at, :] + zgot[j, 2, at, :])
            return carry

        lax.fori_loop(0, 8, rows, 0)

    def send_back(j):
        for k in (2 * j, 2 * j + 1):
            for cs in range(2):
                part = summed.at[j, pl.ds((k - 2 * j) * 64 + cs * 32, 32), :]
                if k == 0:
                    continue
                remote(part, back.at[k, c], back_send.at[k, cs], back_sem.at[k, c],
                       chip(OFFSETS[k], -1) * 2 + cs, z).start()
            if k == 0:
                other = summed.at[0, pl.ds((1 - c) * 32, 32), :]
                remote(other, back.at[0, c], back_send.at[0, 0], back_sem.at[0, c], me + 1 - 2 * c, z).start()
                mine = summed.at[0, pl.ds(c * 32, 32), :]
                pltpu.make_async_copy(mine, back.at[0, c], back_sem.at[0, c]).start()

    def group(j, carry):
        for jj in range(GROUPS):
            @pl.when(j == jj)
            def _():
                if jj + WINDOW < 6:
                    for k in (2 * (jj + WINDOW), 2 * (jj + WINDOW) + 1):
                        pack(k)
                        send(k)
                if jj == 3:
                    forward(0)
                    forward(1)
                if jj == 4:
                    forward(2)
                    forward(3)

        for t in range(2):
            for cs in range(2):
                k = 2 * j + t
                remote(packed.at[0, 0], got.at[k, cs], send_sem.at[0, 0], got_sem.at[k, cs],
                       me + 1 - 2 * c, z).wait_recv()

        def rows(t, carry):
            k, at = 2 * j + t // 4, pl.ds(pl.multiple_of((t % 2) * 16, 16), 16)
            part = got[k, (t // 2) % 2, at, :]
            high = part.astype(jnp.bfloat16)
            to = pl.multiple_of(t * 16, 16)
            lhs[pl.ds(to, 16), :] = high
            lhs[pl.ds(to + 128, 16), :] = (part - high.astype(jnp.float32)).astype(jnp.bfloat16)
            return carry

        lax.fori_loop(0, 8, rows, 0)

        def columns(i, carry):
            layer = lax.rem(z + 1 + i, 4)
            both = jnp.dot(lhs[...], bhi[layer], preferred_element_type=jnp.float32)
            low = jnp.dot(lhs[0:128, :], blo[layer], preferred_element_type=jnp.float32)
            prod[j, i] = both[0:128] + (both[128:256] + low)

            @pl.when(i < 3)
            def _():
                remote(prod.at[j, i], zgot.at[j, i], z_send.at[j, i], z_sem.at[j, i], me, layer).start()

            return carry

        lax.fori_loop(0, 4, columns, 0)

        @pl.when(j > 0)
        def _():
            give_back(j - 1)

        for jj in range(1, GROUPS):
            @pl.when(j == jj)
            def _():
                send_back(jj - 1)

        return carry

    lax.fori_loop(0, GROUPS, group, 0)
    give_back(GROUPS - 1)
    send_back(GROUPS - 1)

    out_ref[...] = jnp.zeros_like(out_ref)
    for k in range(16):
        for oc in range(2):
            remote(summed.at[0, pl.ds(0, 32), :], back.at[k, oc], back_send.at[0, 0], back_sem.at[k, oc],
                   me + 1 - 2 * c, z).wait_recv()
        for oc in range(2):
            one, two = codes(k, oc)
            used = (one < NONE, two > one)
            for s, code in enumerate((one, two)):
                term = back[k, oc, s * ROWS:(s + 1) * ROWS, :]
                for b in range(OBLK):
                    weight = jnp.where(used[s] & (code % OBLK == b), 1.0, 0.0)
                    out_ref[b] += weight * term

    for k in range(16):
        if k >= RELAYED:
            r = k - RELAYED
            remote(packed.at[k], relay.at[r], relay_send.at[r], relay_sem.at[r], me + 1 - 2 * c, z).wait_send()
            for oc in range(2):
                remote(relay.at[r, oc], got.at[k, c], forward_send.at[r, oc], got_sem.at[k, c],
                       me + 1 - 2 * c, z).wait_send()
        else:
            for oc in range(1 if k == 0 else 2):
                remote(packed.at[k, oc], got.at[k, c], send_sem.at[k, oc], got_sem.at[k, c],
                       me + 1 - 2 * c, z).wait_send()
        for cs in range(1 if k == 0 else 2):
            remote(summed.at[0, pl.ds(0, 32), :], back.at[k, c], back_send.at[k, cs], back_sem.at[k, c],
                   me + 1 - 2 * c, z).wait_send()

    def drain(j, carry):
        for i in range(3):
            remote(prod.at[j, i], zgot.at[j, i], z_send.at[j, i], z_sem.at[j, i], me, lax.rem(z + 1, 4)).wait_send()
        return carry

    lax.fori_loop(0, GROUPS, drain, 0)


def shards(amplitudes, tile_occ, tile_virt, owner, integrals):
    slots = amplitudes.shape[0]
    ids = jnp.arange(32, dtype=jnp.int32)
    code = jnp.arange(slots, dtype=jnp.int32) * OBLK + tile_occ
    names = tile_virt[:, 0][:, None] == ids[None, :]
    code0 = jnp.min(jnp.where(names, code[:, None], NONE), axis=0)
    code1 = jnp.max(jnp.where(names, code[:, None], -1), axis=0)
    holds = jnp.sum(jnp.where(owner[:, None] == ids[None, :], ids[:, None], 0), axis=0)
    f32, bf16 = jnp.float32, jnp.bfloat16
    dma = pltpu.SemaphoreType.DMA
    return pl.pallas_call(
        kernel,
        out_shape=jax.ShapeDtypeStruct((OBLK, ROWS, ZCOL), f32),
        in_specs=[pl.BlockSpec(memory_space=pltpu.SMEM)] * 3 + [pl.BlockSpec(memory_space=pl.ANY)] * 2,
        out_specs=pl.BlockSpec(memory_space=pltpu.VMEM),
        scratch_shapes=[
            pltpu.VMEM((slots, ROWS, KDIM), f32),
            pltpu.VMEM((16, 2, 2 * ROWS, KDIM), f32),
            pltpu.VMEM((4, 2, 2 * ROWS, KDIM), f32),
            pltpu.VMEM((16, 2, 2 * ROWS, KDIM), f32),
            pltpu.VMEM((4, KDIM, ZCOL), bf16),
            pltpu.VMEM((4, KDIM, ZCOL), bf16),
            pltpu.VMEM((2, 256, NCOL), f32),
            pltpu.VMEM((256, KDIM), bf16),
            pltpu.VMEM((GROUPS, 4, 128, ZCOL), f32),
            pltpu.VMEM((GROUPS, 3, 128, ZCOL), f32),
            pltpu.VMEM((GROUPS, 128, ZCOL), f32),
            pltpu.VMEM((16, 2, 2 * ROWS, ZCOL), f32),
            dma, dma((2,)), dma((16, 2)), dma((16, 2)), dma((4,)), dma((4,)), dma((4, 2)),
            dma((GROUPS, 3)), dma((GROUPS, 3)), dma((16, 2)), dma((16, 2)),
        ],
        compiler_params=pltpu.CompilerParams(
            collective_id=0, has_side_effects=True, vmem_limit_bytes=64 * 2**20 - 2**17),
        cost_estimate=pl.CostEstimate(
            flops=6 * 1024 * KDIM * NCOL, bytes_accessed=4 * (KDIM * NCOL + slots * ROWS * KDIM), transcendentals=0),
    )(code0, code1, holds, amplitudes, integrals)


def solution(mesh):
    return jax.shard_map(
        shards,
        mesh=mesh,
        in_specs=(P("pair", None, "red"), P("pair"), P("pair", None), P(), P("pair", "red", None)),
        out_specs=P("pair", None, "red"),
        check_vma=False,
    )
```

```python
import functools

import jax
import jax.numpy as jnp
from jax import lax
from jax.experimental import pallas as pl
from jax.experimental.pallas import tpu as pltpu
from jax.sharding import PartitionSpec as P

MESH = pl.DeviceIdType.MESH
OBLK = 4
ROWS = 16
KDIM = 2304
NCOL = 1536
ZCOL = 384
NONE = 1 << 20

OFFSETS = (
    (0, 0), (1, 0),
    (0, 1), (3, 0),
    (0, 3), (1, 1),
    (3, 3), (1, 3),
    (3, 1), (2, 0),
    (0, 2), (2, 2),
    (2, 1), (2, 3),
    (1, 2), (3, 2),
)
GROUPS = 8
RELAYED = 12
RELAY_VIA = ((2, 0), (2, 0), (0, 2), (0, 2))
RELAY_ON = ((0, 1), (0, 3), (1, 0), (3, 0))
LATER = {0: (12, 13, 14, 15), 1: (6, 7), 2: (8, 9), 3: (10, 11)}
ON = {3: (0, 1), 4: (2, 3)}


def split_rows(block, bhi, blo, start, z):
    def rows(t, carry):
        at = pl.multiple_of(t * 16, 16)
        to = pl.ds(pl.multiple_of(start + at, 16), 16)
        for q in range(4):
            part = block[pl.ds(at, 16), q * ZCOL:(q + 1) * ZCOL]
            high = part.astype(jnp.bfloat16)
            slot = lax.rem(q + 3 - z, 4) if q else 3 - z
            half, cols = slot // 2, pl.ds(pl.multiple_of(slot % 2 * ZCOL, 128), ZCOL)
            bhi[half, to, cols] = high
            blo[half, to, cols] = (part - high.astype(jnp.float32)).astype(jnp.bfloat16)
        return carry

    lax.fori_loop(0, 16, rows, 0)


def kernel(code0, code1, holds, amp_hbm, int_hbm, out_ref, spill_ref,
           amp, packed, relay, got, bhi, blo, stage, lhs, prod, zgot, summed, back, over, under, notes, noted,
           amp_sem, stage_sem, send_sem, got_sem, relay_send, relay_sem, forward_send, cross_send,
           z_send, z_sem, back_send, back_sem, over_send, over_sem, note_send, note_sem):
    me = lax.axis_index("pair")
    z = lax.axis_index("red")
    x, y, c = me // 8, (me // 2) % 4, me % 2
    twin = me + 1 - 2 * c

    def device(off, core, sign=1):
        dx, dy = off
        if sign < 0:
            dx, dy = 4 - dx, 4 - dy
        return (lax.rem(x + dx, 4) * 4 + lax.rem(y + dy, 4)) * 2 + core

    def remote(src, dst, ssem, rsem, pair, layer):
        return pltpu.make_async_remote_copy(
            src_ref=src, dst_ref=dst, send_sem=ssem, recv_sem=rsem,
            device_id=(pair, layer), device_id_type=MESH)

    def received(dst, rsem):
        remote(dst, dst, send_sem.at[0, 0], rsem, twin, z).wait_recv()

    def sent(src, ssem):
        remote(src, src, ssem, got_sem.at[0, 0], twin, z).wait_send()

    barrier = pltpu.get_barrier_semaphore()

    def greet(i, carry):
        pl.semaphore_signal(barrier, inc=1, device_id=(lax.rem(me + i, 32), z), device_id_type=MESH)
        return carry

    lax.fori_loop(1, 32, greet, 0)
    for i in range(1, 4):
        pl.semaphore_signal(barrier, inc=1, device_id=(me, lax.rem(z + i, 4)), device_id_type=MESH)

    amp_copy = pltpu.make_async_copy(amp_hbm, amp, amp_sem)
    amp_copy.start()

    def load_stage(i):
        return pltpu.make_async_copy(int_hbm.at[0, pl.ds(i * 256, 256), :], stage.at[i % 2], stage_sem.at[i % 2])

    load_stage(0).start()
    load_stage(1).start()
    amp_copy.wait()

    def codes(k):
        near, far = holds[device(OFFSETS[k], c)], holds[device(OFFSETS[k], 1 - c)]
        return code0[near], code1[near], code0[far], code1[far]

    def pack(k):
        near0, near1, far0, far1 = codes(k)
        second = jnp.where(near1 > near0, near1, jnp.where(far1 > far0, far1, 0))
        packed[k, 0] = amp[jnp.where(far0 < NONE, far0, 0) // OBLK]
        packed[k, 1] = amp[jnp.where(near0 < NONE, near0, 0) // OBLK]
        packed[k, 2] = amp[second // OBLK]

    def send(k):
        if k >= RELAYED:
            r = k - RELAYED
            remote(packed.at[k], relay.at[r], relay_send.at[r], relay_sem.at[r], device(RELAY_VIA[r], c), z).start()
            return
        remote(packed.at[k, 0], got.at[k, 1, 0], send_sem.at[k, 0], got_sem.at[k, 1],
               device(OFFSETS[k], 1 - c), z).start()
        if k == 0:
            pltpu.make_async_copy(packed.at[0, pl.ds(1, 2)], got.at[0, 0], got_sem.at[0, 0]).start()
        else:
            remote(packed.at[k, pl.ds(1, 2)], got.at[k, 0], send_sem.at[k, 1], got_sem.at[k, 0],
                   device(OFFSETS[k], c), z).start()

    def forward(r):
        received(relay.at[r], relay_sem.at[r])
        k = RELAYED + r
        remote(relay.at[r, 0], got.at[k, 1, 0], forward_send.at[r, 0], got_sem.at[k, 1],
               device(RELAY_ON[r], 1 - c), z).start()
        remote(relay.at[r, pl.ds(1, 2)], got.at[k, 0], forward_send.at[r, 1], got_sem.at[k, 0],
               device(RELAY_ON[r], c), z).start()

    for k in range(4):
        pack(k)
    left = jnp.int32(0)
    for k in range(16):
        near0, near1, far0, far1 = codes(k)
        left = left + jnp.where((near1 > near0) & (far1 > far0), 1, 0)
    top = lax.broadcasted_iota(jnp.int32, (8, 128), 0) < 4
    for k in range(16):
        near0, near1, far0, far1 = codes(k)
        mine = jnp.where(near1 > near0, 1.0, 0.0)
        notes[2 * k] = jnp.where(top, mine, left.astype(jnp.float32))
        notes[2 * k + 1] = jnp.where(top, 1.0 - mine, left.astype(jnp.float32))
    pl.semaphore_wait(barrier, 34)
    for k in range(16):
        remote(notes.at[2 * k + 1], noted.at[2 * k + 1], note_send, note_sem, device(OFFSETS[k], 1 - c), z).start()
        if k == 0:
            noted[0] = notes[0]
        else:
            remote(notes.at[2 * k], noted.at[2 * k], note_send, note_sem, device(OFFSETS[k], c), z).start()
    for k in range(4):
        send(k)
    for k in range(4, 6):
        pack(k)
        send(k)

    for i in range(9):
        load_stage(i).wait()
        split_rows(stage.at[i % 2], bhi, blo, i * 256, z)
        if i + 2 < 9:
            load_stage(i + 2).start()

    received(noted.at[pl.ds(1, 31)], note_sem)

    def share_group(j):
        received(under.at[j], over_sem.at[j])
        for n in range(4):
            prod[j, n, 64:96, :] += under[j, :, n * ZCOL:(n + 1) * ZCOL]
            if n < 3:
                remote(prod.at[j, n], zgot.at[j, n], z_send.at[j, n], z_sem.at[j, n], me, lax.rem(z + 1 + n, 4)).start()

    def reduce_group(j):
        for i in range(3):
            received(zgot.at[j, i], z_sem.at[j, i])
        for role in range(3):
            for t in range(2):
                at = slice(role * 32 + t * 16, role * 32 + t * 16 + 16)
                summed[j, t, (0, 2, 1)[role]] = (prod[j, 3, at, :] + zgot[j, 0, at, :]) + (zgot[j, 1, at, :] + zgot[j, 2, at, :])

    def send_back(j):
        for t in range(2):
            k = 2 * j + t
            near, far = summed.at[j, t, pl.ds(0, 2)], summed.at[j, t, 2]
            remote(far, back.at[k, 2], back_send.at[k, 1], back_sem.at[k, 1], device(OFFSETS[k], 1 - c, -1), z).start()
            if k == 0:
                pltpu.make_async_copy(near, back.at[0, pl.ds(0, 2)], back_sem.at[0, 0]).start()
            else:
                remote(near, back.at[k, pl.ds(0, 2)], back_send.at[k, 0], back_sem.at[k, 0],
                       device(OFFSETS[k], c, -1), z).start()

    def group(j, carry):
        for jj in range(GROUPS):
            @pl.when(j == jj)
            def _():
                for k in LATER.get(jj, ()):
                    pack(k)
                    send(k)
                for r in ON.get(jj, ()):
                    forward(r)

        for t in range(2):
            k = 2 * j + t
            received(got.at[k, 0], got_sem.at[k, 0])
            remote(got.at[k, 0, 1], got.at[k, 1, 1], cross_send.at[k], got_sem.at[k, 2], twin, z).start()
        for t in range(2):
            k = 2 * j + t
            received(got.at[k, 1, 0], got_sem.at[k, 1])
            received(got.at[k, 1, 1], got_sem.at[k, 2])

        def place(t, part):
            high = part.astype(jnp.bfloat16)
            to = pl.multiple_of(t * 16, 16)
            lhs[pl.ds(to, 16), :] = high
            lhs[pl.ds(to + 128, 16), :] = (part - high.astype(jnp.float32)).astype(jnp.bfloat16)

        def first_tiles(t, carry):
            place(t, got[2 * j + t % 2, t // 2, 0])
            return carry

        def second_tiles(t, carry):
            k, side = 2 * j + t % 2, t // 2
            place(t + 4, got[k, side, 1] * noted[2 * k + side, 0:1, 0:1])
            return carry

        lax.fori_loop(0, 4, first_tiles, 0)
        lax.fori_loop(0, 4, second_tiles, 0)

        @pl.when(j > 0)
        def _():
            share_group(j - 1)

        def columns(i, carry):
            both = jnp.dot(lhs[...], bhi[i], preferred_element_type=jnp.float32)
            low = jnp.dot(lhs[0:128, :], blo[i], preferred_element_type=jnp.float32)
            term = both[0:128] + (both[128:256] + low)
            prod[j, 2 * i] = term[0:96, 0:ZCOL]
            prod[j, 2 * i + 1] = term[0:96, ZCOL:2 * ZCOL]
            over[j, :, pl.ds(pl.multiple_of(i * 2 * ZCOL, 128), 2 * ZCOL)] = term[96:128]
            return carry

        lax.fori_loop(0, 2, columns, 0)
        remote(over.at[j], under.at[j], over_send.at[j], over_sem.at[j], twin, z).start()

        @pl.when(j > 1)
        def _():
            reduce_group(j - 2)

        for jj in range(2, GROUPS):
            @pl.when(j == jj)
            def _():
                send_back(jj - 2)

        return carry

    lax.fori_loop(0, GROUPS, group, 0)
    share_group(GROUPS - 1)
    for j in (GROUPS - 2, GROUPS - 1):
        reduce_group(j)
        send_back(j)

    out_ref[...] = jnp.zeros_like(out_ref)
    for k in range(16):
        near0, near1, far0, far1 = codes(k)
        second = jnp.where(near1 > near0, near1, far1)
        tiles = ((near0, near0 < NONE), (second, (near1 > near0) | (far1 > far0)), (far0, far0 < NONE))
        received(back.at[k, pl.ds(0, 2)], back_sem.at[k, 0])
        received(back.at[k, 2], back_sem.at[k, 1])
        for s, (code, used) in enumerate(tiles):
            term = back[k, s]
            for b in range(OBLK):
                weight = jnp.where(used & (code % OBLK == b), 1.0, 0.0)
                out_ref[b] += weight * term

    spill = noted[0]
    for i in range(1, 32):
        spill = jnp.maximum(spill, noted[i])
    spill_ref[...] = spill

    for k in range(16):
        if k >= RELAYED:
            r = k - RELAYED
            sent(packed.at[k], relay_send.at[r])
            sent(relay.at[r, 0], forward_send.at[r, 0])
            sent(relay.at[r, pl.ds(1, 2)], forward_send.at[r, 1])
        else:
            sent(packed.at[k, 0], send_sem.at[k, 0])
            if k > 0:
                sent(packed.at[k, pl.ds(1, 2)], send_sem.at[k, 1])
        sent(got.at[k, 0, 1], cross_send.at[k])
        sent(back.at[k, 2], back_send.at[k, 1])
        if k > 0:
            sent(back.at[k, pl.ds(0, 2)], back_send.at[k, 0])

    def drain(j, carry):
        for i in range(3):
            sent(prod.at[j, i], z_send.at[j, i])
        sent(over.at[j], over_send.at[j])
        return carry

    lax.fori_loop(0, GROUPS, drain, 0)
    sent(notes.at[pl.ds(1, 31)], note_send)


def spill_kernel(code0, code1, holds, amp_hbm, int_hbm, start_ref, out_ref,
                 amp, packed, got, bhi, blo, stage, lhs, prod, zgot, summed, back,
                 amp_sem, stage_sem, send_sem, got_sem, z_send, z_sem, back_send, back_sem):
    me = lax.axis_index("pair")
    z = lax.axis_index("red")
    x, y, c = me // 8, (me // 2) % 4, me % 2

    def device(off, core, sign=1):
        dx, dy = off
        if sign < 0:
            dx, dy = 4 - dx, 4 - dy
        return (lax.rem(x + dx, 4) * 4 + lax.rem(y + dy, 4)) * 2 + core

    def remote(src, dst, ssem, rsem, pair, layer):
        return pltpu.make_async_remote_copy(
            src_ref=src, dst_ref=dst, send_sem=ssem, recv_sem=rsem,
            device_id=(pair, layer), device_id_type=MESH)

    def received(dst, rsem):
        remote(dst, dst, send_sem.at[0], rsem, me + 1 - 2 * c, z).wait_recv()

    def sent(src, ssem):
        remote(src, src, ssem, got_sem.at[0], me + 1 - 2 * c, z).wait_send()

    barrier = pltpu.get_barrier_semaphore()

    def greet(i, carry):
        pl.semaphore_signal(barrier, inc=1, device_id=(2 * i + 1 - c, z), device_id_type=MESH)
        return carry

    lax.fori_loop(0, 16, greet, 0)
    for i in range(1, 4):
        pl.semaphore_signal(barrier, inc=1, device_id=(me, lax.rem(z + i, 4)), device_id_type=MESH)

    amp_copy = pltpu.make_async_copy(amp_hbm, amp, amp_sem)
    amp_copy.start()

    def load_stage(i):
        return pltpu.make_async_copy(int_hbm.at[0, pl.ds(i * 256, 256), :], stage.at[i % 2], stage_sem.at[i % 2])

    load_stage(0).start()
    load_stage(1).start()
    amp_copy.wait()

    def spilled(k):
        near, far = holds[device(OFFSETS[k], c)], holds[device(OFFSETS[k], 1 - c)]
        return code1[far], (code1[near] > code0[near]) & (code1[far] > code0[far])

    for k in range(16):
        code, used = spilled(k)
        packed[k] = amp[jnp.where(used, code, 0) // OBLK]
    pl.semaphore_wait(barrier, 19)
    for k in range(16):
        remote(packed.at[k], got.at[k], send_sem.at[k], got_sem.at[k], device(OFFSETS[k], 1 - c), z).start()

    for i in range(9):
        load_stage(i).wait()
        split_rows(stage.at[i % 2], bhi, blo, i * 256, z)
        if i + 2 < 9:
            load_stage(i + 2).start()

    for j in range(2):
        for k in range(8 * j, 8 * j + 8):
            received(got.at[k], got_sem.at[k])

        def rows(t, carry):
            part = got[8 * j + t]
            high = part.astype(jnp.bfloat16)
            to = pl.multiple_of(t * 16, 16)
            lhs[pl.ds(to, 16), :] = high
            lhs[pl.ds(to + 128, 16), :] = (part - high.astype(jnp.float32)).astype(jnp.bfloat16)
            return carry

        lax.fori_loop(0, 8, rows, 0)

        def columns(i, carry):
            both = jnp.dot(lhs[...], bhi[i], preferred_element_type=jnp.float32)
            low = jnp.dot(lhs[0:128, :], blo[i], preferred_element_type=jnp.float32)
            term = both[0:128] + (both[128:256] + low)
            prod[j, 2 * i] = term[:, 0:ZCOL]
            prod[j, 2 * i + 1] = term[:, ZCOL:2 * ZCOL]
            return carry

        lax.fori_loop(0, 2, columns, 0)
        for n in range(3):
            remote(prod.at[j, n], zgot.at[j, n], z_send.at[j, n], z_sem.at[j, n], me, lax.rem(z + 1 + n, 4)).start()

    for j in range(2):
        for n in range(3):
            received(zgot.at[j, n], z_sem.at[j, n])
        for t in range(8):
            k, at = 8 * j + t, slice(t * 16, t * 16 + 16)
            summed[k] = (prod[j, 3, at, :] + zgot[j, 0, at, :]) + (zgot[j, 1, at, :] + zgot[j, 2, at, :])
            remote(summed.at[k], back.at[k], back_send.at[k], back_sem.at[k], device(OFFSETS[k], 1 - c, -1), z).start()

    out_ref[...] = start_ref[...]
    for k in range(16):
        code, used = spilled(k)
        received(back.at[k], back_sem.at[k])
        for b in range(OBLK):
            weight = jnp.where(used & (code % OBLK == b), 1.0, 0.0)
            out_ref[b] += weight * back[k]

    for k in range(16):
        sent(packed.at[k], send_sem.at[k])
        sent(summed.at[k], back_send.at[k])
    for j in range(2):
        for n in range(3):
            sent(prod.at[j, n], z_send.at[j, n])


def shards(amplitudes, tile_occ, tile_virt, owner, integrals):
    slots = amplitudes.shape[0]
    ids = jnp.arange(32, dtype=jnp.int32)
    code = jnp.arange(slots, dtype=jnp.int32) * OBLK + tile_occ
    names = tile_virt[:, 0][:, None] == ids[None, :]
    code0 = jnp.min(jnp.where(names, code[:, None], NONE), axis=0)
    code1 = jnp.max(jnp.where(names, code[:, None], -1), axis=0)
    holds = jnp.sum(jnp.where(owner[:, None] == ids[None, :], ids[:, None], 0), axis=0)
    f32, bf16 = jnp.float32, jnp.bfloat16
    dma = pltpu.SemaphoreType.DMA
    out, spill = pl.pallas_call(
        kernel,
        out_shape=(jax.ShapeDtypeStruct((OBLK, ROWS, ZCOL), f32), jax.ShapeDtypeStruct((8, 128), f32)),
        in_specs=[pl.BlockSpec(memory_space=pltpu.SMEM)] * 3 + [pl.BlockSpec(memory_space=pl.ANY)] * 2,
        out_specs=(pl.BlockSpec(memory_space=pltpu.VMEM),) * 2,
        scratch_shapes=[
            pltpu.VMEM((slots, ROWS, KDIM), f32),
            pltpu.VMEM((16, 3, ROWS, KDIM), f32),
            pltpu.VMEM((4, 3, ROWS, KDIM), f32),
            pltpu.VMEM((16, 2, 2, ROWS, KDIM), f32),
            pltpu.VMEM((2, KDIM, 2 * ZCOL), bf16),
            pltpu.VMEM((2, KDIM, 2 * ZCOL), bf16),
            pltpu.VMEM((2, 256, NCOL), f32),
            pltpu.VMEM((256, KDIM), bf16),
            pltpu.VMEM((GROUPS, 4, 96, ZCOL), f32),
            pltpu.VMEM((GROUPS, 3, 96, ZCOL), f32),
            pltpu.VMEM((GROUPS, 2, 3, ROWS, ZCOL), f32),
            pltpu.VMEM((16, 3, ROWS, ZCOL), f32),
            pltpu.VMEM((GROUPS, 32, NCOL), f32),
            pltpu.VMEM((GROUPS, 32, NCOL), f32),
            pltpu.VMEM((32, 8, 128), f32),
            pltpu.VMEM((32, 8, 128), f32),
            dma, dma((2,)), dma((16, 2)), dma((16, 3)), dma((4,)), dma((4,)), dma((4, 2)), dma((16,)),
            dma((GROUPS, 3)), dma((GROUPS, 3)), dma((16, 2)), dma((16, 2)), dma((GROUPS,)), dma((GROUPS,)), dma, dma,
        ],
        compiler_params=pltpu.CompilerParams(
            collective_id=0, has_side_effects=True, vmem_limit_bytes=64 * 2**20 - 2**17),
        cost_estimate=pl.CostEstimate(
            flops=6 * 1024 * KDIM * NCOL, bytes_accessed=4 * (KDIM * NCOL + slots * ROWS * KDIM), transcendentals=0),
    )(code0, code1, holds, amplitudes, integrals)

    def add_spilled(first):
        return pl.pallas_call(
            spill_kernel,
            out_shape=jax.ShapeDtypeStruct((OBLK, ROWS, ZCOL), f32),
            in_specs=[pl.BlockSpec(memory_space=pltpu.SMEM)] * 3 + [pl.BlockSpec(memory_space=pl.ANY)] * 2
            + [pl.BlockSpec(memory_space=pltpu.VMEM)],
            out_specs=pl.BlockSpec(memory_space=pltpu.VMEM),
            scratch_shapes=[
                pltpu.VMEM((slots, ROWS, KDIM), f32),
                pltpu.VMEM((16, ROWS, KDIM), f32),
                pltpu.VMEM((16, ROWS, KDIM), f32),
                pltpu.VMEM((2, KDIM, 2 * ZCOL), bf16),
                pltpu.VMEM((2, KDIM, 2 * ZCOL), bf16),
                pltpu.VMEM((2, 256, NCOL), f32),
                pltpu.VMEM((256, KDIM), bf16),
                pltpu.VMEM((2, 4, 128, ZCOL), f32),
                pltpu.VMEM((2, 3, 128, ZCOL), f32),
                pltpu.VMEM((16, ROWS, ZCOL), f32),
                pltpu.VMEM((16, ROWS, ZCOL), f32),
                dma, dma((2,)), dma((16,)), dma((16,)), dma((2, 3)), dma((2, 3)), dma((16,)), dma((16,)),
            ],
            compiler_params=pltpu.CompilerParams(
                collective_id=1, has_side_effects=True, vmem_limit_bytes=60 * 2**20),
            cost_estimate=pl.CostEstimate(
                flops=6 * 256 * KDIM * NCOL, bytes_accessed=4 * (KDIM * NCOL + slots * ROWS * KDIM), transcendentals=0),
        )(code0, code1, holds, amplitudes, integrals, first)

    return lax.cond(spill[7, 0] > 0.0, add_spilled, lambda first: first, out)


def solution(mesh):
    return jax.shard_map(
        shards,
        mesh=mesh,
        in_specs=(P("pair", None, "red"), P("pair"), P("pair", None), P(), P("pair", "red", None)),
        out_specs=P("pair", None, "red"),
        check_vma=False,
    )
```

```python
import functools

import jax
import jax.numpy as jnp
from jax import lax
from jax.experimental import pallas as pl
from jax.experimental.pallas import tpu as pltpu
from jax.sharding import PartitionSpec as P

MESH = pl.DeviceIdType.MESH
OBLK = 4
ROWS = 16
KDIM = 2304
NCOL = 1536
ZCOL = 384
NONE = 1 << 20

OFFSETS = (
    (0, 0), (1, 0), (0, 1), (3, 0), (0, 3),
    (1, 1), (3, 3), (1, 3), (3, 1),
    (2, 0), (0, 2),
    (2, 1), (2, 3), (1, 2), (3, 2),
    (2, 2),
)
STEPS = 16
LAG = 3
PROMPT = 13
RELAYED, RELAYS = 11, 4
RELAY_VIA = ((2, 0), (2, 0), (0, 2), (0, 2))
RELAY_ON = ((0, 1), (0, 3), (1, 0), (3, 0))
EARLY = (0, 1, 2, 3, 4)
MEANWHILE = {3: (5, 6), 5: (7, 8)}
LATER = {1: (11, 12, 13, 14), 5: (9, 10), 8: (15,)}
ON = {7: (0, 1, 2, 3)}


def split_rows(block, bhi, blo, start, z):
    def rows(t, carry):
        at = pl.multiple_of(t * 32, 32)
        to = pl.ds(pl.multiple_of(start + at, 32), 32)
        parts = [block[pl.ds(at, 32), q * ZCOL:(q + 1) * ZCOL] for q in range(4)]
        high = [part.astype(jnp.bfloat16) for part in parts]
        low = [(part - top.astype(jnp.float32)).astype(jnp.bfloat16) for part, top in zip(parts, high)]
        for q in range(4):
            slot = lax.rem(q + 3 - z, 4) if q else 3 - z
            half, cols = slot // 2, pl.ds(pl.multiple_of(slot % 2 * ZCOL, 128), ZCOL)
            bhi[half, to, cols] = high[q]
            blo[half, to, cols] = low[q]
        return carry

    lax.fori_loop(0, 8, rows, 0)


def kernel(code0, code1, holds, amp_hbm, int_hbm, out_ref, spill_ref,
           amp, packed, relay, got, bhi, blo, stage, lhs, prod, zgot, summed, back, over, under, notes, noted,
           amp_sem, stage_sem, send_sem, got_sem, relay_send, relay_sem, forward_send, cross_send,
           z_send, z_sem, back_send, back_sem, over_send, over_sem, note_send, note_sem):
    me = lax.axis_index("pair")
    z = lax.axis_index("red")
    x, y, c = me // 8, (me // 2) % 4, me % 2
    twin = me + 1 - 2 * c

    def device(off, core, sign=1):
        dx, dy = off
        if sign < 0:
            dx, dy = 4 - dx, 4 - dy
        return (lax.rem(x + dx, 4) * 4 + lax.rem(y + dy, 4)) * 2 + core

    def remote(src, dst, ssem, rsem, pair, layer):
        return pltpu.make_async_remote_copy(
            src_ref=src, dst_ref=dst, send_sem=ssem, recv_sem=rsem,
            device_id=(pair, layer), device_id_type=MESH)

    def received(dst, rsem):
        remote(dst, dst, send_sem.at[0, 0], rsem, twin, z).wait_recv()

    def sent(src, ssem):
        remote(src, src, ssem, got_sem.at[0, 0], twin, z).wait_send()

    barrier = pltpu.get_barrier_semaphore()

    def greet(i, carry):
        pl.semaphore_signal(barrier, inc=1, device_id=(lax.rem(me + i, 32), z), device_id_type=MESH)
        return carry

    lax.fori_loop(1, 32, greet, 0)
    for i in range(1, 4):
        pl.semaphore_signal(barrier, inc=1, device_id=(me, lax.rem(z + i, 4)), device_id_type=MESH)

    amp_copy = pltpu.make_async_copy(amp_hbm, amp, amp_sem)
    amp_copy.start()

    def load_stage(i):
        return pltpu.make_async_copy(int_hbm.at[0, pl.ds(i * 256, 256), :], stage.at[i % 2], stage_sem.at[i % 2])

    load_stage(0).start()
    load_stage(1).start()
    amp_copy.wait()

    def codes(k):
        near, far = holds[device(OFFSETS[k], c)], holds[device(OFFSETS[k], 1 - c)]
        return code0[near], code1[near], code0[far], code1[far]

    def pack(k):
        near0, near1, far0, far1 = codes(k)
        second = jnp.where(near1 > near0, near1, jnp.where(far1 > far0, far1, 0))
        packed[k, 0] = amp[jnp.where(far0 < NONE, far0, 0) // OBLK]
        packed[k, 1] = amp[jnp.where(near0 < NONE, near0, 0) // OBLK]
        packed[k, 2] = amp[second // OBLK]

    def send(k):
        if RELAYED <= k < RELAYED + RELAYS:
            r = k - RELAYED
            remote(packed.at[k], relay.at[r], relay_send.at[r], relay_sem.at[r], device(RELAY_VIA[r], c), z).start()
            return
        remote(packed.at[k, 0], got.at[k, 1, 0], send_sem.at[k, 0], got_sem.at[k, 1],
               device(OFFSETS[k], 1 - c), z).start()
        if k == 0:
            pltpu.make_async_copy(packed.at[0, pl.ds(1, 2)], got.at[0, 0], got_sem.at[0, 0]).start()
        else:
            remote(packed.at[k, pl.ds(1, 2)], got.at[k, 0], send_sem.at[k, 1], got_sem.at[k, 0],
                   device(OFFSETS[k], c), z).start()

    def forward(r):
        received(relay.at[r], relay_sem.at[r])
        k = RELAYED + r
        remote(relay.at[r, 0], got.at[k, 1, 0], forward_send.at[r, 0], got_sem.at[k, 1],
               device(RELAY_ON[r], 1 - c), z).start()
        remote(relay.at[r, pl.ds(1, 2)], got.at[k, 0], forward_send.at[r, 1], got_sem.at[k, 0],
               device(RELAY_ON[r], c), z).start()

    for k in EARLY:
        pack(k)
    left = jnp.int32(0)
    for k in range(16):
        near0, near1, far0, far1 = codes(k)
        left = left + jnp.where((near1 > near0) & (far1 > far0), 1, 0)
    top = lax.broadcasted_iota(jnp.int32, (8, 128), 0) < 4
    for k in range(16):
        near0, near1, far0, far1 = codes(k)
        mine = jnp.where(near1 > near0, 1.0, 0.0)
        notes[2 * k] = jnp.where(top, mine, left.astype(jnp.float32))
        notes[2 * k + 1] = jnp.where(top, 1.0 - mine, left.astype(jnp.float32))
    pl.semaphore_wait(barrier, 34)
    for k in range(16):
        remote(notes.at[2 * k + 1], noted.at[2 * k + 1], note_send, note_sem, device(OFFSETS[k], 1 - c), z).start()
        if k == 0:
            noted[0] = notes[0]
        else:
            remote(notes.at[2 * k], noted.at[2 * k], note_send, note_sem, device(OFFSETS[k], c), z).start()
    for k in EARLY:
        send(k)

    for i in range(9):
        load_stage(i).wait()
        split_rows(stage.at[i % 2], bhi, blo, i * 256, z)
        if i + 2 < 9:
            load_stage(i + 2).start()
        for k in MEANWHILE.get(i, ()):
            pack(k)
            send(k)

    received(noted.at[pl.ds(1, 31)], note_sem)

    def share(j):
        received(under.at[j], over_sem.at[j])
        for n in range(4):
            prod[j, n, 32:48, :] += under[j, :, n * ZCOL:(n + 1) * ZCOL]
            if n < 3:
                remote(prod.at[j, n], zgot.at[j, n], z_send.at[j, n], z_sem.at[j, n], me, lax.rem(z + 1 + n, 4)).start()

    def reduce_step(j):
        for i in range(3):
            received(zgot.at[j, i], z_sem.at[j, i])
        for role in range(3):
            at = slice(role * 16, role * 16 + 16)
            summed[j, (0, 2, 1)[role]] = (prod[j, 3, at, :] + zgot[j, 0, at, :]) + (zgot[j, 1, at, :] + zgot[j, 2, at, :])

    def send_back(k):
        near, far = summed.at[k, pl.ds(0, 2)], summed.at[k, 2]
        remote(far, back.at[k, 2], back_send.at[k, 1], back_sem.at[k, 1], device(OFFSETS[k], 1 - c, -1), z).start()
        if k == 0:
            pltpu.make_async_copy(near, back.at[0, pl.ds(0, 2)], back_sem.at[0, 0]).start()
        else:
            remote(near, back.at[k, pl.ds(0, 2)], back_send.at[k, 0], back_sem.at[k, 0],
                   device(OFFSETS[k], c, -1), z).start()

    def step(j, carry):
        for jj in range(STEPS):
            @pl.when(j == jj)
            def _():
                for k in LATER.get(jj, ()):
                    pack(k)
                    send(k)
                for r in ON.get(jj, ()):
                    forward(r)

        received(got.at[j, 0], got_sem.at[j, 0])
        remote(got.at[j, 0, 1], got.at[j, 1, 1], cross_send.at[j], got_sem.at[j, 2], twin, z).start()

        def place(t, part):
            high = part.astype(jnp.bfloat16)
            lhs[t * 16:t * 16 + 16, :] = high
            lhs[t * 16 + 64:t * 16 + 80, :] = (part - high.astype(jnp.float32)).astype(jnp.bfloat16)

        place(0, got[j, 0, 0])
        place(2, got[j, 0, 1] * noted[2 * j, 0:1, 0:1])
        received(got.at[j, 1, 0], got_sem.at[j, 1])
        place(1, got[j, 1, 0])
        received(got.at[j, 1, 1], got_sem.at[j, 2])
        place(3, got[j, 1, 1] * noted[2 * j + 1, 0:1, 0:1])

        @pl.when((j > 0) & (j <= PROMPT))
        def _():
            share(j - 1)

        def columns(i, carry):
            both = jnp.dot(lhs[...], bhi[i], preferred_element_type=jnp.float32)
            low = jnp.dot(lhs[0:64, :], blo[i], preferred_element_type=jnp.float32)
            term = both[0:64] + (both[64:128] + low)
            prod[j, 2 * i] = term[0:48, 0:ZCOL]
            prod[j, 2 * i + 1] = term[0:48, ZCOL:2 * ZCOL]
            over[j, :, pl.ds(pl.multiple_of(i * 2 * ZCOL, 128), 2 * ZCOL)] = term[48:64]
            return carry

        lax.fori_loop(0, 2, columns, 0)
        remote(over.at[j], under.at[j], over_send.at[j], over_sem.at[j], twin, z).start()

        @pl.when(j >= LAG)
        def _():
            reduce_step(j - LAG)

        for jj in range(LAG, STEPS):
            @pl.when(j == jj)
            def _():
                send_back(jj - LAG)

        @pl.when(j >= PROMPT)
        def _():
            share(j)

        return carry

    lax.fori_loop(0, STEPS, step, 0)
    for j in range(STEPS - LAG, STEPS):
        reduce_step(j)
        send_back(j)

    total = [jnp.zeros((ROWS, ZCOL), jnp.float32) for b in range(OBLK)]
    for k in range(16):
        near0, near1, far0, far1 = codes(k)
        second = jnp.where(near1 > near0, near1, far1)
        tiles = ((near0, near0 < NONE), (second, (near1 > near0) | (far1 > far0)), (far0, far0 < NONE))
        received(back.at[k, pl.ds(0, 2)], back_sem.at[k, 0])
        received(back.at[k, 2], back_sem.at[k, 1])
        for s, (code, used) in enumerate(tiles):
            term = back[k, s]
            for b in range(OBLK):
                weight = jnp.where(used & (code % OBLK == b), 1.0, 0.0)
                total[b] = total[b] + weight * term
    for b in range(OBLK):
        out_ref[b] = total[b]

    spill = noted[0]
    for i in range(1, 32):
        spill = jnp.maximum(spill, noted[i])
    spill_ref[...] = spill

    for k in range(16):
        if RELAYED <= k < RELAYED + RELAYS:
            r = k - RELAYED
            sent(packed.at[k], relay_send.at[r])
            sent(relay.at[r, 0], forward_send.at[r, 0])
            sent(relay.at[r, pl.ds(1, 2)], forward_send.at[r, 1])
        else:
            sent(packed.at[k, 0], send_sem.at[k, 0])
            if k > 0:
                sent(packed.at[k, pl.ds(1, 2)], send_sem.at[k, 1])
        sent(got.at[k, 0, 1], cross_send.at[k])
        sent(back.at[k, 2], back_send.at[k, 1])
        if k > 0:
            sent(back.at[k, pl.ds(0, 2)], back_send.at[k, 0])

    def drain(j, carry):
        for i in range(3):
            sent(prod.at[j, i], z_send.at[j, i])
        sent(over.at[j], over_send.at[j])
        return carry

    lax.fori_loop(0, STEPS, drain, 0)
    sent(notes.at[pl.ds(1, 31)], note_send)


def spill_kernel(code0, code1, holds, amp_hbm, int_hbm, start_ref, out_ref,
                 amp, packed, got, bhi, blo, stage, lhs, prod, zgot, summed, back,
                 amp_sem, stage_sem, send_sem, got_sem, z_send, z_sem, back_send, back_sem):
    me = lax.axis_index("pair")
    z = lax.axis_index("red")
    x, y, c = me // 8, (me // 2) % 4, me % 2

    def device(off, core, sign=1):
        dx, dy = off
        if sign < 0:
            dx, dy = 4 - dx, 4 - dy
        return (lax.rem(x + dx, 4) * 4 + lax.rem(y + dy, 4)) * 2 + core

    def remote(src, dst, ssem, rsem, pair, layer):
        return pltpu.make_async_remote_copy(
            src_ref=src, dst_ref=dst, send_sem=ssem, recv_sem=rsem,
            device_id=(pair, layer), device_id_type=MESH)

    def received(dst, rsem):
        remote(dst, dst, send_sem.at[0], rsem, me + 1 - 2 * c, z).wait_recv()

    def sent(src, ssem):
        remote(src, src, ssem, got_sem.at[0], me + 1 - 2 * c, z).wait_send()

    barrier = pltpu.get_barrier_semaphore()

    def greet(i, carry):
        pl.semaphore_signal(barrier, inc=1, device_id=(2 * i + 1 - c, z), device_id_type=MESH)
        return carry

    lax.fori_loop(0, 16, greet, 0)
    for i in range(1, 4):
        pl.semaphore_signal(barrier, inc=1, device_id=(me, lax.rem(z + i, 4)), device_id_type=MESH)

    amp_copy = pltpu.make_async_copy(amp_hbm, amp, amp_sem)
    amp_copy.start()

    def load_stage(i):
        return pltpu.make_async_copy(int_hbm.at[0, pl.ds(i * 256, 256), :], stage.at[i % 2], stage_sem.at[i % 2])

    load_stage(0).start()
    load_stage(1).start()
    amp_copy.wait()

    def spilled(k):
        near, far = holds[device(OFFSETS[k], c)], holds[device(OFFSETS[k], 1 - c)]
        return code1[far], (code1[near] > code0[near]) & (code1[far] > code0[far])

    for k in range(16):
        code, used = spilled(k)
        packed[k] = amp[jnp.where(used, code, 0) // OBLK]
    pl.semaphore_wait(barrier, 19)
    for k in range(16):
        remote(packed.at[k], got.at[k], send_sem.at[k], got_sem.at[k], device(OFFSETS[k], 1 - c), z).start()

    for i in range(9):
        load_stage(i).wait()
        split_rows(stage.at[i % 2], bhi, blo, i * 256, z)
        if i + 2 < 9:
            load_stage(i + 2).start()

    def finish(j):
        for n in range(3):
            received(zgot.at[j, n], z_sem.at[j, n])
        for t in range(4):
            k, at = 4 * j + t, slice(t * 16, t * 16 + 16)
            summed[k] = (prod[j, 3, at, :] + zgot[j, 0, at, :]) + (zgot[j, 1, at, :] + zgot[j, 2, at, :])
            remote(summed.at[k], back.at[k], back_send.at[k], back_sem.at[k], device(OFFSETS[k], 1 - c, -1), z).start()

    for j in range(4):
        for t in range(4):
            k = 4 * j + t
            received(got.at[k], got_sem.at[k])
            part = got[k]
            high = part.astype(jnp.bfloat16)
            lhs[t * 16:t * 16 + 16, :] = high
            lhs[t * 16 + 64:t * 16 + 80, :] = (part - high.astype(jnp.float32)).astype(jnp.bfloat16)

        def columns(i, carry):
            both = jnp.dot(lhs[...], bhi[i], preferred_element_type=jnp.float32)
            low = jnp.dot(lhs[0:64, :], blo[i], preferred_element_type=jnp.float32)
            term = both[0:64] + (both[64:128] + low)
            prod[j, 2 * i] = term[:, 0:ZCOL]
            prod[j, 2 * i + 1] = term[:, ZCOL:2 * ZCOL]
            return carry

        lax.fori_loop(0, 2, columns, 0)
        for n in range(3):
            remote(prod.at[j, n], zgot.at[j, n], z_send.at[j, n], z_sem.at[j, n], me, lax.rem(z + 1 + n, 4)).start()
        if j:
            finish(j - 1)
    finish(3)

    out_ref[...] = start_ref[...]
    for k in range(16):
        code, used = spilled(k)
        received(back.at[k], back_sem.at[k])
        for b in range(OBLK):
            weight = jnp.where(used & (code % OBLK == b), 1.0, 0.0)
            out_ref[b] += weight * back[k]

    for k in range(16):
        sent(packed.at[k], send_sem.at[k])
        sent(summed.at[k], back_send.at[k])
    for j in range(4):
        for n in range(3):
            sent(prod.at[j, n], z_send.at[j, n])


def shards(amplitudes, tile_occ, tile_virt, owner, integrals):
    slots = amplitudes.shape[0]
    ids = jnp.arange(32, dtype=jnp.int32)
    code = jnp.arange(slots, dtype=jnp.int32) * OBLK + tile_occ
    names = tile_virt[:, 0][:, None] == ids[None, :]
    code0 = jnp.min(jnp.where(names, code[:, None], NONE), axis=0)
    code1 = jnp.max(jnp.where(names, code[:, None], -1), axis=0)
    holds = jnp.sum(jnp.where(owner[:, None] == ids[None, :], ids[:, None], 0), axis=0)
    f32, bf16 = jnp.float32, jnp.bfloat16
    dma = pltpu.SemaphoreType.DMA
    out, spill = pl.pallas_call(
        kernel,
        out_shape=(jax.ShapeDtypeStruct((OBLK, ROWS, ZCOL), f32), jax.ShapeDtypeStruct((8, 128), f32)),
        in_specs=[pl.BlockSpec(memory_space=pltpu.SMEM)] * 3 + [pl.BlockSpec(memory_space=pl.ANY)] * 2,
        out_specs=(pl.BlockSpec(memory_space=pltpu.VMEM),) * 2,
        scratch_shapes=[
            pltpu.VMEM((slots, ROWS, KDIM), f32),
            pltpu.VMEM((16, 3, ROWS, KDIM), f32),
            pltpu.VMEM((4, 3, ROWS, KDIM), f32),
            pltpu.VMEM((16, 2, 2, ROWS, KDIM), f32),
            pltpu.VMEM((2, KDIM, 2 * ZCOL), bf16),
            pltpu.VMEM((2, KDIM, 2 * ZCOL), bf16),
            pltpu.VMEM((2, 256, NCOL), f32),
            pltpu.VMEM((128, KDIM), bf16),
            pltpu.VMEM((STEPS, 4, 48, ZCOL), f32),
            pltpu.VMEM((STEPS, 3, 48, ZCOL), f32),
            pltpu.VMEM((STEPS, 3, ROWS, ZCOL), f32),
            pltpu.VMEM((16, 3, ROWS, ZCOL), f32),
            pltpu.VMEM((STEPS, ROWS, NCOL), f32),
            pltpu.VMEM((STEPS, ROWS, NCOL), f32),
            pltpu.VMEM((32, 8, 128), f32),
            pltpu.VMEM((32, 8, 128), f32),
            dma, dma((2,)), dma((16, 2)), dma((16, 3)), dma((4,)), dma((4,)), dma((4, 2)), dma((16,)),
            dma((STEPS, 3)), dma((STEPS, 3)), dma((16, 2)), dma((16, 2)), dma((STEPS,)), dma((STEPS,)), dma, dma,
        ],
        compiler_params=pltpu.CompilerParams(
            collective_id=0, has_side_effects=True, vmem_limit_bytes=64 * 2**20 - 2**17),
        cost_estimate=pl.CostEstimate(
            flops=6 * 1024 * KDIM * NCOL, bytes_accessed=4 * (KDIM * NCOL + slots * ROWS * KDIM), transcendentals=0),
    )(code0, code1, holds, amplitudes, integrals)

    def add_spilled(first):
        return pl.pallas_call(
            spill_kernel,
            out_shape=jax.ShapeDtypeStruct((OBLK, ROWS, ZCOL), f32),
            in_specs=[pl.BlockSpec(memory_space=pltpu.SMEM)] * 3 + [pl.BlockSpec(memory_space=pl.ANY)] * 2
            + [pl.BlockSpec(memory_space=pltpu.VMEM)],
            out_specs=pl.BlockSpec(memory_space=pltpu.VMEM),
            scratch_shapes=[
                pltpu.VMEM((slots, ROWS, KDIM), f32),
                pltpu.VMEM((16, ROWS, KDIM), f32),
                pltpu.VMEM((16, ROWS, KDIM), f32),
                pltpu.VMEM((2, KDIM, 2 * ZCOL), bf16),
                pltpu.VMEM((2, KDIM, 2 * ZCOL), bf16),
                pltpu.VMEM((2, 256, NCOL), f32),
                pltpu.VMEM((128, KDIM), bf16),
                pltpu.VMEM((4, 4, 64, ZCOL), f32),
                pltpu.VMEM((4, 3, 64, ZCOL), f32),
                pltpu.VMEM((16, ROWS, ZCOL), f32),
                pltpu.VMEM((16, ROWS, ZCOL), f32),
                dma, dma((2,)), dma((16,)), dma((16,)), dma((4, 3)), dma((4, 3)), dma((16,)), dma((16,)),
            ],
            compiler_params=pltpu.CompilerParams(
                collective_id=1, has_side_effects=True, vmem_limit_bytes=60 * 2**20),
            cost_estimate=pl.CostEstimate(
                flops=6 * 256 * KDIM * NCOL, bytes_accessed=4 * (KDIM * NCOL + slots * ROWS * KDIM), transcendentals=0),
        )(code0, code1, holds, amplitudes, integrals, first)

    return lax.cond(spill[7, 0] > 0.0, add_spilled, lambda first: first, out)


def solution(mesh):
    return jax.shard_map(
        shards,
        mesh=mesh,
        in_specs=(P("pair", None, "red"), P("pair"), P("pair", None), P(), P("pair", "red", None)),
        out_specs=P("pair", None, "red"),
        check_vma=False,
    )
```

```python
import functools

import jax
import jax.numpy as jnp
from jax import lax
from jax.experimental import pallas as pl
from jax.experimental.pallas import tpu as pltpu
from jax.sharding import PartitionSpec as P

MESH = pl.DeviceIdType.MESH
OBLK = 4
ROWS = 16
KDIM = 2304
NCOL = 1536
ZCOL = 384
NONE = 1 << 20

OFFSETS = (
    (0, 0), (1, 0), (0, 1), (3, 0), (0, 3),
    (1, 1), (3, 3), (1, 3), (3, 1),
    (2, 0), (0, 2),
    (2, 1), (2, 3), (1, 2), (3, 2),
    (2, 2),
)
STEPS = 16
LAG = 3
PROMPT = 15
RELAYED, RELAYS = 11, 4
RELAY_VIA = ((2, 0), (2, 0), (0, 2), (0, 2))
RELAY_ON = ((0, 1), (0, 3), (1, 0), (3, 0))
EARLY = (0, 1, 2, 3, 4)
MEANWHILE = {3: (5, 6), 5: (7, 8)}
LATER = {1: (11, 12, 13, 14), 5: (9, 10), 8: (15,)}
ON = {7: (0, 1, 2, 3)}


def split_rows(block, bhi, blo, start, z):
    def rows(t, carry):
        at = pl.multiple_of(t * 32, 32)
        to = pl.ds(pl.multiple_of(start + at, 32), 32)
        parts = [block[pl.ds(at, 32), q * ZCOL:(q + 1) * ZCOL] for q in range(4)]
        high = [part.astype(jnp.bfloat16) for part in parts]
        low = [(part - top.astype(jnp.float32)).astype(jnp.bfloat16) for part, top in zip(parts, high)]
        for q in range(4):
            slot = lax.rem(q + 3 - z, 4) if q else 3 - z
            half, cols = slot // 2, pl.ds(pl.multiple_of(slot % 2 * ZCOL, 128), ZCOL)
            bhi[half, to, cols] = high[q]
            blo[half, to, cols] = low[q]
        return carry

    lax.fori_loop(0, 8, rows, 0)


def kernel(code0, code1, holds, amp_hbm, int_hbm, out_ref, spill_ref,
           amp, packed, relay, got, bhi, blo, stage, lhs, prod, zgot, summed, back, over, under, notes, noted,
           amp_sem, stage_sem, send_sem, got_sem, relay_send, relay_sem, forward_send, cross_send,
           z_send, z_sem, back_send, back_sem, over_send, over_sem, note_send, note_sem):
    me = lax.axis_index("pair")
    z = lax.axis_index("red")
    x, y, c = me // 8, (me // 2) % 4, me % 2
    twin = me + 1 - 2 * c

    def device(off, core, sign=1):
        dx, dy = off
        if sign < 0:
            dx, dy = 4 - dx, 4 - dy
        return (lax.rem(x + dx, 4) * 4 + lax.rem(y + dy, 4)) * 2 + core

    def remote(src, dst, ssem, rsem, pair, layer):
        return pltpu.make_async_remote_copy(
            src_ref=src, dst_ref=dst, send_sem=ssem, recv_sem=rsem,
            device_id=(pair, layer), device_id_type=MESH)

    def received(dst, rsem):
        remote(dst, dst, send_sem.at[0, 0], rsem, twin, z).wait_recv()

    def sent(src, ssem):
        remote(src, src, ssem, got_sem.at[0, 0], twin, z).wait_send()

    barrier = pltpu.get_barrier_semaphore()

    def greet(i, carry):
        pl.semaphore_signal(barrier, inc=1, device_id=(lax.rem(me + i, 32), z), device_id_type=MESH)
        return carry

    lax.fori_loop(1, 32, greet, 0)
    for i in range(1, 4):
        pl.semaphore_signal(barrier, inc=1, device_id=(me, lax.rem(z + i, 4)), device_id_type=MESH)

    amp_copy = pltpu.make_async_copy(amp_hbm, amp, amp_sem)
    amp_copy.start()

    def load_stage(i):
        return pltpu.make_async_copy(int_hbm.at[0, pl.ds(i * 256, 256), :], stage.at[i % 2], stage_sem.at[i % 2])

    load_stage(0).start()
    load_stage(1).start()
    amp_copy.wait()

    def codes(k):
        near, far = holds[device(OFFSETS[k], c)], holds[device(OFFSETS[k], 1 - c)]
        return code0[near], code1[near], code0[far], code1[far]

    def pack(k):
        near0, near1, far0, far1 = codes(k)
        second = jnp.where(near1 > near0, near1, jnp.where(far1 > far0, far1, 0))
        packed[k, 0] = amp[jnp.where(far0 < NONE, far0, 0) // OBLK]
        packed[k, 1] = amp[jnp.where(near0 < NONE, near0, 0) // OBLK]
        packed[k, 2] = amp[second // OBLK]

    def send(k):
        if RELAYED <= k < RELAYED + RELAYS:
            r = k - RELAYED
            remote(packed.at[k], relay.at[r], relay_send.at[r], relay_sem.at[r], device(RELAY_VIA[r], c), z).start()
            return
        remote(packed.at[k, 0], got.at[k, 1, 0], send_sem.at[k, 0], got_sem.at[k, 1],
               device(OFFSETS[k], 1 - c), z).start()
        if k == 0:
            pltpu.make_async_copy(packed.at[0, pl.ds(1, 2)], got.at[0, 0], got_sem.at[0, 0]).start()
        else:
            remote(packed.at[k, pl.ds(1, 2)], got.at[k, 0], send_sem.at[k, 1], got_sem.at[k, 0],
                   device(OFFSETS[k], c), z).start()

    def forward(r):
        received(relay.at[r], relay_sem.at[r])
        k = RELAYED + r
        remote(relay.at[r, 0], got.at[k, 1, 0], forward_send.at[r, 0], got_sem.at[k, 1],
               device(RELAY_ON[r], 1 - c), z).start()
        remote(relay.at[r, pl.ds(1, 2)], got.at[k, 0], forward_send.at[r, 1], got_sem.at[k, 0],
               device(RELAY_ON[r], c), z).start()

    for k in EARLY:
        pack(k)
    pl.semaphore_wait(barrier, 34)
    for k in EARLY:
        send(k)
    left = jnp.int32(0)
    for k in range(16):
        near0, near1, far0, far1 = codes(k)
        left = left + jnp.where((near1 > near0) & (far1 > far0), 1, 0)
    top = lax.broadcasted_iota(jnp.int32, (8, 128), 0) < 4
    for k in range(16):
        near0, near1, far0, far1 = codes(k)
        mine = jnp.where(near1 > near0, 1.0, 0.0)
        notes[2 * k] = jnp.where(top, mine, left.astype(jnp.float32))
        notes[2 * k + 1] = jnp.where(top, 1.0 - mine, left.astype(jnp.float32))
    for k in range(16):
        remote(notes.at[2 * k + 1], noted.at[2 * k + 1], note_send, note_sem, device(OFFSETS[k], 1 - c), z).start()
        if k == 0:
            noted[0] = notes[0]
        else:
            remote(notes.at[2 * k], noted.at[2 * k], note_send, note_sem, device(OFFSETS[k], c), z).start()

    for i in range(9):
        load_stage(i).wait()
        split_rows(stage.at[i % 2], bhi, blo, i * 256, z)
        if i + 2 < 9:
            load_stage(i + 2).start()
        for k in MEANWHILE.get(i, ()):
            pack(k)
            send(k)

    received(noted.at[pl.ds(1, 31)], note_sem)

    def share(j):
        received(under.at[j], over_sem.at[j])
        for n in range(4):
            prod[j, n, 32:48, :] += under[j, :, n * ZCOL:(n + 1) * ZCOL]
            if n < 3:
                remote(prod.at[j, n], zgot.at[j, n], z_send.at[j, n], z_sem.at[j, n], me, lax.rem(z + 1 + n, 4)).start()

    def reduce_step(j):
        for i in range(3):
            received(zgot.at[j, i], z_sem.at[j, i])
        for role in range(3):
            at = slice(role * 16, role * 16 + 16)
            summed[j, (0, 2, 1)[role]] = (prod[j, 3, at, :] + zgot[j, 0, at, :]) + (zgot[j, 1, at, :] + zgot[j, 2, at, :])

    def send_back(k):
        near, far = summed.at[k, pl.ds(0, 2)], summed.at[k, 2]
        remote(far, back.at[k, 2], back_send.at[k, 1], back_sem.at[k, 1], device(OFFSETS[k], 1 - c, -1), z).start()
        if k == 0:
            pltpu.make_async_copy(near, back.at[0, pl.ds(0, 2)], back_sem.at[0, 0]).start()
        else:
            remote(near, back.at[k, pl.ds(0, 2)], back_send.at[k, 0], back_sem.at[k, 0],
                   device(OFFSETS[k], c, -1), z).start()

    def step(j, carry):
        for jj in range(STEPS):
            @pl.when(j == jj)
            def _():
                for k in LATER.get(jj, ()):
                    pack(k)
                    send(k)
                for r in ON.get(jj, ()):
                    forward(r)

        received(got.at[j, 0], got_sem.at[j, 0])
        remote(got.at[j, 0, 1], got.at[j, 1, 1], cross_send.at[j], got_sem.at[j, 2], twin, z).start()

        def place(t, part):
            high = part.astype(jnp.bfloat16)
            lhs[t * 16:t * 16 + 16, :] = high
            lhs[t * 16 + 64:t * 16 + 80, :] = (part - high.astype(jnp.float32)).astype(jnp.bfloat16)

        place(0, got[j, 0, 0])
        place(2, got[j, 0, 1] * noted[2 * j, 0:1, 0:1])
        received(got.at[j, 1, 0], got_sem.at[j, 1])
        place(1, got[j, 1, 0])
        received(got.at[j, 1, 1], got_sem.at[j, 2])
        place(3, got[j, 1, 1] * noted[2 * j + 1, 0:1, 0:1])

        @pl.when((j > 0) & (j <= PROMPT))
        def _():
            share(j - 1)

        def columns(i, carry):
            both = jnp.dot(lhs[...], bhi[i], preferred_element_type=jnp.float32)
            low = jnp.dot(lhs[0:64, :], blo[i], preferred_element_type=jnp.float32)
            term = both[0:64] + (both[64:128] + low)
            prod[j, 2 * i] = term[0:48, 0:ZCOL]
            prod[j, 2 * i + 1] = term[0:48, ZCOL:2 * ZCOL]
            over[j, :, pl.ds(pl.multiple_of(i * 2 * ZCOL, 128), 2 * ZCOL)] = term[48:64]
            return carry

        lax.fori_loop(0, 2, columns, 0)
        remote(over.at[j], under.at[j], over_send.at[j], over_sem.at[j], twin, z).start()

        @pl.when(j >= LAG)
        def _():
            reduce_step(j - LAG)

        for jj in range(LAG, STEPS):
            @pl.when(j == jj)
            def _():
                send_back(jj - LAG)

        @pl.when(j >= PROMPT)
        def _():
            share(j)

        return carry

    lax.fori_loop(0, STEPS, step, 0)
    for j in range(STEPS - LAG, STEPS):
        reduce_step(j)
        send_back(j)

    total = [jnp.zeros((ROWS, ZCOL), jnp.float32) for b in range(OBLK)]
    for k in range(16):
        near0, near1, far0, far1 = codes(k)
        second = jnp.where(near1 > near0, near1, far1)
        tiles = ((near0, near0 < NONE), (second, (near1 > near0) | (far1 > far0)), (far0, far0 < NONE))
        received(back.at[k, pl.ds(0, 2)], back_sem.at[k, 0])
        received(back.at[k, 2], back_sem.at[k, 1])
        for s, (code, used) in enumerate(tiles):
            term = back[k, s]
            for b in range(OBLK):
                weight = jnp.where(used & (code % OBLK == b), 1.0, 0.0)
                total[b] = total[b] + weight * term
    for b in range(OBLK):
        out_ref[b] = total[b]

    spill = noted[0]
    for i in range(1, 32):
        spill = jnp.maximum(spill, noted[i])
    spill_ref[...] = spill

    for k in range(16):
        if RELAYED <= k < RELAYED + RELAYS:
            r = k - RELAYED
            sent(packed.at[k], relay_send.at[r])
            sent(relay.at[r, 0], forward_send.at[r, 0])
            sent(relay.at[r, pl.ds(1, 2)], forward_send.at[r, 1])
        else:
            sent(packed.at[k, 0], send_sem.at[k, 0])
            if k > 0:
                sent(packed.at[k, pl.ds(1, 2)], send_sem.at[k, 1])
        sent(got.at[k, 0, 1], cross_send.at[k])
        sent(back.at[k, 2], back_send.at[k, 1])
        if k > 0:
            sent(back.at[k, pl.ds(0, 2)], back_send.at[k, 0])

    def drain(j, carry):
        for i in range(3):
            sent(prod.at[j, i], z_send.at[j, i])
        sent(over.at[j], over_send.at[j])
        return carry

    lax.fori_loop(0, STEPS, drain, 0)
    sent(notes.at[pl.ds(1, 31)], note_send)


def spill_kernel(code0, code1, holds, amp_hbm, int_hbm, start_ref, out_ref,
                 amp, packed, got, bhi, blo, stage, lhs, prod, zgot, summed, back,
                 amp_sem, stage_sem, send_sem, got_sem, z_send, z_sem, back_send, back_sem):
    me = lax.axis_index("pair")
    z = lax.axis_index("red")
    x, y, c = me // 8, (me // 2) % 4, me % 2

    def device(off, core, sign=1):
        dx, dy = off
        if sign < 0:
            dx, dy = 4 - dx, 4 - dy
        return (lax.rem(x + dx, 4) * 4 + lax.rem(y + dy, 4)) * 2 + core

    def remote(src, dst, ssem, rsem, pair, layer):
        return pltpu.make_async_remote_copy(
            src_ref=src, dst_ref=dst, send_sem=ssem, recv_sem=rsem,
            device_id=(pair, layer), device_id_type=MESH)

    def received(dst, rsem):
        remote(dst, dst, send_sem.at[0], rsem, me + 1 - 2 * c, z).wait_recv()

    def sent(src, ssem):
        remote(src, src, ssem, got_sem.at[0], me + 1 - 2 * c, z).wait_send()

    barrier = pltpu.get_barrier_semaphore()

    def greet(i, carry):
        pl.semaphore_signal(barrier, inc=1, device_id=(2 * i + 1 - c, z), device_id_type=MESH)
        return carry

    lax.fori_loop(0, 16, greet, 0)
    for i in range(1, 4):
        pl.semaphore_signal(barrier, inc=1, device_id=(me, lax.rem(z + i, 4)), device_id_type=MESH)

    amp_copy = pltpu.make_async_copy(amp_hbm, amp, amp_sem)
    amp_copy.start()

    def load_stage(i):
        return pltpu.make_async_copy(int_hbm.at[0, pl.ds(i * 256, 256), :], stage.at[i % 2], stage_sem.at[i % 2])

    load_stage(0).start()
    load_stage(1).start()
    amp_copy.wait()

    def spilled(k):
        near, far = holds[device(OFFSETS[k], c)], holds[device(OFFSETS[k], 1 - c)]
        return code1[far], (code1[near] > code0[near]) & (code1[far] > code0[far])

    for k in range(16):
        code, used = spilled(k)
        packed[k] = amp[jnp.where(used, code, 0) // OBLK]
    pl.semaphore_wait(barrier, 19)
    for k in range(16):
        remote(packed.at[k], got.at[k], send_sem.at[k], got_sem.at[k], device(OFFSETS[k], 1 - c), z).start()

    for i in range(9):
        load_stage(i).wait()
        split_rows(stage.at[i % 2], bhi, blo, i * 256, z)
        if i + 2 < 9:
            load_stage(i + 2).start()

    def finish(j):
        for n in range(3):
            received(zgot.at[j, n], z_sem.at[j, n])
        for t in range(4):
            k, at = 4 * j + t, slice(t * 16, t * 16 + 16)
            summed[k] = (prod[j, 3, at, :] + zgot[j, 0, at, :]) + (zgot[j, 1, at, :] + zgot[j, 2, at, :])
            remote(summed.at[k], back.at[k], back_send.at[k], back_sem.at[k], device(OFFSETS[k], 1 - c, -1), z).start()

    for j in range(4):
        for t in range(4):
            k = 4 * j + t
            received(got.at[k], got_sem.at[k])
            part = got[k]
            high = part.astype(jnp.bfloat16)
            lhs[t * 16:t * 16 + 16, :] = high
            lhs[t * 16 + 64:t * 16 + 80, :] = (part - high.astype(jnp.float32)).astype(jnp.bfloat16)

        def columns(i, carry):
            both = jnp.dot(lhs[...], bhi[i], preferred_element_type=jnp.float32)
            low = jnp.dot(lhs[0:64, :], blo[i], preferred_element_type=jnp.float32)
            term = both[0:64] + (both[64:128] + low)
            prod[j, 2 * i] = term[:, 0:ZCOL]
            prod[j, 2 * i + 1] = term[:, ZCOL:2 * ZCOL]
            return carry

        lax.fori_loop(0, 2, columns, 0)
        for n in range(3):
            remote(prod.at[j, n], zgot.at[j, n], z_send.at[j, n], z_sem.at[j, n], me, lax.rem(z + 1 + n, 4)).start()
        if j:
            finish(j - 1)
    finish(3)

    out_ref[...] = start_ref[...]
    for k in range(16):
        code, used = spilled(k)
        received(back.at[k], back_sem.at[k])
        for b in range(OBLK):
            weight = jnp.where(used & (code % OBLK == b), 1.0, 0.0)
            out_ref[b] += weight * back[k]

    for k in range(16):
        sent(packed.at[k], send_sem.at[k])
        sent(summed.at[k], back_send.at[k])
    for j in range(4):
        for n in range(3):
            sent(prod.at[j, n], z_send.at[j, n])


def shards(amplitudes, tile_occ, tile_virt, owner, integrals):
    slots = amplitudes.shape[0]
    ids = jnp.arange(32, dtype=jnp.int32)
    code = jnp.arange(slots, dtype=jnp.int32) * OBLK + tile_occ
    names = tile_virt[:, 0][:, None] == ids[None, :]
    code0 = jnp.min(jnp.where(names, code[:, None], NONE), axis=0)
    code1 = jnp.max(jnp.where(names, code[:, None], -1), axis=0)
    holds = jnp.sum(jnp.where(owner[:, None] == ids[None, :], ids[:, None], 0), axis=0)
    f32, bf16 = jnp.float32, jnp.bfloat16
    dma = pltpu.SemaphoreType.DMA
    out, spill = pl.pallas_call(
        kernel,
        out_shape=(jax.ShapeDtypeStruct((OBLK, ROWS, ZCOL), f32), jax.ShapeDtypeStruct((8, 128), f32)),
        in_specs=[pl.BlockSpec(memory_space=pltpu.SMEM)] * 3 + [pl.BlockSpec(memory_space=pl.ANY)] * 2,
        out_specs=(pl.BlockSpec(memory_space=pltpu.VMEM),) * 2,
        scratch_shapes=[
            pltpu.VMEM((slots, ROWS, KDIM), f32),
            pltpu.VMEM((16, 3, ROWS, KDIM), f32),
            pltpu.VMEM((4, 3, ROWS, KDIM), f32),
            pltpu.VMEM((16, 2, 2, ROWS, KDIM), f32),
            pltpu.VMEM((2, KDIM, 2 * ZCOL), bf16),
            pltpu.VMEM((2, KDIM, 2 * ZCOL), bf16),
            pltpu.VMEM((2, 256, NCOL), f32),
            pltpu.VMEM((128, KDIM), bf16),
            pltpu.VMEM((STEPS, 4, 48, ZCOL), f32),
            pltpu.VMEM((STEPS, 3, 48, ZCOL), f32),
            pltpu.VMEM((STEPS, 3, ROWS, ZCOL), f32),
            pltpu.VMEM((16, 3, ROWS, ZCOL), f32),
            pltpu.VMEM((STEPS, ROWS, NCOL), f32),
            pltpu.VMEM((STEPS, ROWS, NCOL), f32),
            pltpu.VMEM((32, 8, 128), f32),
            pltpu.VMEM((32, 8, 128), f32),
            dma, dma((2,)), dma((16, 2)), dma((16, 3)), dma((4,)), dma((4,)), dma((4, 2)), dma((16,)),
            dma((STEPS, 3)), dma((STEPS, 3)), dma((16, 2)), dma((16, 2)), dma((STEPS,)), dma((STEPS,)), dma, dma,
        ],
        compiler_params=pltpu.CompilerParams(
            collective_id=0, has_side_effects=True, vmem_limit_bytes=64 * 2**20 - 2**17),
        cost_estimate=pl.CostEstimate(
            flops=6 * 1024 * KDIM * NCOL, bytes_accessed=4 * (KDIM * NCOL + slots * ROWS * KDIM), transcendentals=0),
    )(code0, code1, holds, amplitudes, integrals)

    def add_spilled(first):
        return pl.pallas_call(
            spill_kernel,
            out_shape=jax.ShapeDtypeStruct((OBLK, ROWS, ZCOL), f32),
            in_specs=[pl.BlockSpec(memory_space=pltpu.SMEM)] * 3 + [pl.BlockSpec(memory_space=pl.ANY)] * 2
            + [pl.BlockSpec(memory_space=pltpu.VMEM)],
            out_specs=pl.BlockSpec(memory_space=pltpu.VMEM),
            scratch_shapes=[
                pltpu.VMEM((slots, ROWS, KDIM), f32),
                pltpu.VMEM((16, ROWS, KDIM), f32),
                pltpu.VMEM((16, ROWS, KDIM), f32),
                pltpu.VMEM((2, KDIM, 2 * ZCOL), bf16),
                pltpu.VMEM((2, KDIM, 2 * ZCOL), bf16),
                pltpu.VMEM((2, 256, NCOL), f32),
                pltpu.VMEM((128, KDIM), bf16),
                pltpu.VMEM((4, 4, 64, ZCOL), f32),
                pltpu.VMEM((4, 3, 64, ZCOL), f32),
                pltpu.VMEM((16, ROWS, ZCOL), f32),
                pltpu.VMEM((16, ROWS, ZCOL), f32),
                dma, dma((2,)), dma((16,)), dma((16,)), dma((4, 3)), dma((4, 3)), dma((16,)), dma((16,)),
            ],
            compiler_params=pltpu.CompilerParams(
                collective_id=1, has_side_effects=True, vmem_limit_bytes=60 * 2**20),
            cost_estimate=pl.CostEstimate(
                flops=6 * 256 * KDIM * NCOL, bytes_accessed=4 * (KDIM * NCOL + slots * ROWS * KDIM), transcendentals=0),
        )(code0, code1, holds, amplitudes, integrals, first)

    return lax.cond(spill[7, 0] > 0.0, add_spilled, lambda first: first, out)


def solution(mesh):
    return jax.shard_map(
        shards,
        mesh=mesh,
        in_specs=(P("pair", None, "red"), P("pair"), P("pair", None), P(), P("pair", "red", None)),
        out_specs=P("pair", None, "red"),
        check_vma=False,
    )
```

```python
import functools

import jax
import jax.numpy as jnp
from jax import lax
from jax.experimental import pallas as pl
from jax.experimental.pallas import tpu as pltpu
from jax.sharding import PartitionSpec as P

MESH = pl.DeviceIdType.MESH
OBLK = 4
ROWS = 16
KDIM = 2304
NCOL = 1536
ZCOL = 384
NONE = 1 << 20

OFFSETS = (
    (0, 0), (1, 0), (0, 1), (3, 0), (0, 3),
    (1, 1), (3, 3), (1, 3), (3, 1),
    (2, 0), (0, 2),
    (2, 1), (2, 3), (1, 2), (3, 2),
    (2, 2),
)
STEPS = 16
LAG = 4
PROMPT = 15
RELAYED, RELAYS = 11, 4
RELAY_VIA = ((2, 0), (2, 0), (0, 2), (0, 2))
RELAY_ON = ((0, 1), (0, 3), (1, 0), (3, 0))
EARLY = (0, 1, 2, 3, 4)
MEANWHILE = {3: (5, 6), 5: (7, 8)}
LATER = {1: (11, 12, 13, 14), 5: (9, 10), 8: (15,)}
ON = {7: (0, 1, 2, 3)}


def split_rows(block, bhi, blo, start, z):
    def rows(t, carry):
        at = pl.multiple_of(t * 32, 32)
        to = pl.ds(pl.multiple_of(start + at, 32), 32)
        parts = [block[pl.ds(at, 32), q * ZCOL:(q + 1) * ZCOL] for q in range(4)]
        high = [part.astype(jnp.bfloat16) for part in parts]
        low = [(part - top.astype(jnp.float32)).astype(jnp.bfloat16) for part, top in zip(parts, high)]
        for q in range(4):
            slot = lax.rem(q + 3 - z, 4) if q else 3 - z
            half, cols = slot // 2, pl.ds(pl.multiple_of(slot % 2 * ZCOL, 128), ZCOL)
            bhi[half, to, cols] = high[q]
            blo[half, to, cols] = low[q]
        return carry

    lax.fori_loop(0, 8, rows, 0)


def kernel(code0, code1, holds, amp_hbm, int_hbm, out_ref, spill_ref,
           amp, packed, relay, got, bhi, blo, stage, lhs, prod, zgot, summed, back, over, under, notes, noted,
           amp_sem, stage_sem, send_sem, got_sem, relay_send, relay_sem, forward_send, cross_send,
           z_send, z_sem, back_send, back_sem, over_send, over_sem, note_send, note_sem):
    me = lax.axis_index("pair")
    z = lax.axis_index("red")
    x, y, c = me // 8, (me // 2) % 4, me % 2
    twin = me + 1 - 2 * c

    def device(off, core, sign=1):
        dx, dy = off
        if sign < 0:
            dx, dy = 4 - dx, 4 - dy
        return (lax.rem(x + dx, 4) * 4 + lax.rem(y + dy, 4)) * 2 + core

    def remote(src, dst, ssem, rsem, pair, layer):
        return pltpu.make_async_remote_copy(
            src_ref=src, dst_ref=dst, send_sem=ssem, recv_sem=rsem,
            device_id=(pair, layer), device_id_type=MESH)

    def received(dst, rsem):
        remote(dst, dst, send_sem.at[0, 0], rsem, twin, z).wait_recv()

    def sent(src, ssem):
        remote(src, src, ssem, got_sem.at[0, 0], twin, z).wait_send()

    barrier = pltpu.get_barrier_semaphore()

    def greet(i, carry):
        pl.semaphore_signal(barrier, inc=1, device_id=(lax.rem(me + i, 32), z), device_id_type=MESH)
        return carry

    lax.fori_loop(1, 32, greet, 0)
    for i in range(1, 4):
        pl.semaphore_signal(barrier, inc=1, device_id=(me, lax.rem(z + i, 4)), device_id_type=MESH)

    amp_copy = pltpu.make_async_copy(amp_hbm, amp, amp_sem)
    amp_copy.start()

    def load_stage(i):
        return pltpu.make_async_copy(int_hbm.at[0, pl.ds(i * 256, 256), :], stage.at[i % 2], stage_sem.at[i % 2])

    load_stage(0).start()
    load_stage(1).start()
    amp_copy.wait()

    def codes(k):
        near, far = holds[device(OFFSETS[k], c)], holds[device(OFFSETS[k], 1 - c)]
        return code0[near], code1[near], code0[far], code1[far]

    def pack(k):
        near0, near1, far0, far1 = codes(k)
        second = jnp.where(near1 > near0, near1, jnp.where(far1 > far0, far1, 0))
        packed[k, 0] = amp[jnp.where(far0 < NONE, far0, 0) // OBLK]
        packed[k, 1] = amp[jnp.where(near0 < NONE, near0, 0) // OBLK]
        packed[k, 2] = amp[second // OBLK]

    def send(k):
        if RELAYED <= k < RELAYED + RELAYS:
            r = k - RELAYED
            remote(packed.at[k], relay.at[r], relay_send.at[r], relay_sem.at[r], device(RELAY_VIA[r], c), z).start()
            return
        remote(packed.at[k, 0], got.at[k, 1, 0], send_sem.at[k, 0], got_sem.at[k, 1],
               device(OFFSETS[k], 1 - c), z).start()
        if k == 0:
            pltpu.make_async_copy(packed.at[0, pl.ds(1, 2)], got.at[0, 0], got_sem.at[0, 0]).start()
        else:
            remote(packed.at[k, pl.ds(1, 2)], got.at[k, 0], send_sem.at[k, 1], got_sem.at[k, 0],
                   device(OFFSETS[k], c), z).start()

    def forward(r):
        received(relay.at[r], relay_sem.at[r])
        k = RELAYED + r
        remote(relay.at[r, 0], got.at[k, 1, 0], forward_send.at[r, 0], got_sem.at[k, 1],
               device(RELAY_ON[r], 1 - c), z).start()
        remote(relay.at[r, pl.ds(1, 2)], got.at[k, 0], forward_send.at[r, 1], got_sem.at[k, 0],
               device(RELAY_ON[r], c), z).start()

    for k in EARLY:
        pack(k)
    pl.semaphore_wait(barrier, 34)
    for k in EARLY:
        send(k)
    left = jnp.int32(0)
    for k in range(16):
        near0, near1, far0, far1 = codes(k)
        left = left + jnp.where((near1 > near0) & (far1 > far0), 1, 0)
    top = lax.broadcasted_iota(jnp.int32, (8, 128), 0) < 4
    for k in range(16):
        near0, near1, far0, far1 = codes(k)
        mine = jnp.where(near1 > near0, 1.0, 0.0)
        notes[2 * k] = jnp.where(top, mine, left.astype(jnp.float32))
        notes[2 * k + 1] = jnp.where(top, 1.0 - mine, left.astype(jnp.float32))
    for k in range(16):
        remote(notes.at[2 * k + 1], noted.at[2 * k + 1], note_send, note_sem, device(OFFSETS[k], 1 - c), z).start()
        if k == 0:
            noted[0] = notes[0]
        else:
            remote(notes.at[2 * k], noted.at[2 * k], note_send, note_sem, device(OFFSETS[k], c), z).start()

    for i in range(9):
        load_stage(i).wait()
        split_rows(stage.at[i % 2], bhi, blo, i * 256, z)
        if i + 2 < 9:
            load_stage(i + 2).start()
        for k in MEANWHILE.get(i, ()):
            pack(k)
            send(k)

    received(noted.at[pl.ds(1, 31)], note_sem)

    def share(j):
        received(under.at[j], over_sem.at[j])
        for n in range(4):
            prod[j, n, 32:48, :] += under[j, :, n * ZCOL:(n + 1) * ZCOL]
            if n < 3:
                remote(prod.at[j, n], zgot.at[j, n], z_send.at[j, n], z_sem.at[j, n], me, lax.rem(z + 1 + n, 4)).start()

    def reduce_step(j):
        for i in range(3):
            received(zgot.at[j, i], z_sem.at[j, i])
        for role in range(3):
            at = slice(role * 16, role * 16 + 16)
            summed[j, (0, 2, 1)[role]] = (prod[j, 3, at, :] + zgot[j, 0, at, :]) + (zgot[j, 1, at, :] + zgot[j, 2, at, :])

    def send_back(k):
        near, far = summed.at[k, pl.ds(0, 2)], summed.at[k, 2]
        remote(far, back.at[k, 2], back_send.at[k, 1], back_sem.at[k, 1], device(OFFSETS[k], 1 - c, -1), z).start()
        if k == 0:
            pltpu.make_async_copy(near, back.at[0, pl.ds(0, 2)], back_sem.at[0, 0]).start()
        else:
            remote(near, back.at[k, pl.ds(0, 2)], back_send.at[k, 0], back_sem.at[k, 0],
                   device(OFFSETS[k], c, -1), z).start()

    def step(j, carry):
        for jj in range(STEPS):
            @pl.when(j == jj)
            def _():
                for k in LATER.get(jj, ()):
                    pack(k)
                    send(k)
                for r in ON.get(jj, ()):
                    forward(r)

        received(got.at[j, 0], got_sem.at[j, 0])
        remote(got.at[j, 0, 1], got.at[j, 1, 1], cross_send.at[j], got_sem.at[j, 2], twin, z).start()

        def place(t, part):
            high = part.astype(jnp.bfloat16)
            lhs[t * 16:t * 16 + 16, :] = high
            lhs[t * 16 + 64:t * 16 + 80, :] = (part - high.astype(jnp.float32)).astype(jnp.bfloat16)

        place(0, got[j, 0, 0])
        place(2, got[j, 0, 1] * noted[2 * j, 0:1, 0:1])
        received(got.at[j, 1, 0], got_sem.at[j, 1])
        place(1, got[j, 1, 0])
        received(got.at[j, 1, 1], got_sem.at[j, 2])
        place(3, got[j, 1, 1] * noted[2 * j + 1, 0:1, 0:1])

        @pl.when((j > 0) & (j <= PROMPT))
        def _():
            share(j - 1)

        def columns(i, carry):
            both = jnp.dot(lhs[...], bhi[i], preferred_element_type=jnp.float32)
            low = jnp.dot(lhs[0:64, :], blo[i], preferred_element_type=jnp.float32)
            term = both[0:64] + (both[64:128] + low)
            prod[j, 2 * i] = term[0:48, 0:ZCOL]
            prod[j, 2 * i + 1] = term[0:48, ZCOL:2 * ZCOL]
            over[j, :, pl.ds(pl.multiple_of(i * 2 * ZCOL, 128), 2 * ZCOL)] = term[48:64]
            return carry

        lax.fori_loop(0, 2, columns, 0)
        remote(over.at[j], under.at[j], over_send.at[j], over_sem.at[j], twin, z).start()

        @pl.when(j >= LAG)
        def _():
            reduce_step(j - LAG)

        for jj in range(LAG, STEPS):
            @pl.when(j == jj)
            def _():
                send_back(jj - LAG)

        @pl.when(j >= PROMPT)
        def _():
            share(j)

        return carry

    lax.fori_loop(0, STEPS, step, 0)
    for j in range(STEPS - LAG, STEPS):
        reduce_step(j)
        send_back(j)

    total = [jnp.zeros((ROWS, ZCOL), jnp.float32) for b in range(OBLK)]
    for k in range(16):
        near0, near1, far0, far1 = codes(k)
        second = jnp.where(near1 > near0, near1, far1)
        tiles = ((near0, near0 < NONE), (second, (near1 > near0) | (far1 > far0)), (far0, far0 < NONE))
        received(back.at[k, pl.ds(0, 2)], back_sem.at[k, 0])
        received(back.at[k, 2], back_sem.at[k, 1])
        for s, (code, used) in enumerate(tiles):
            term = back[k, s]
            for b in range(OBLK):
                weight = jnp.where(used & (code % OBLK == b), 1.0, 0.0)
                total[b] = total[b] + weight * term
    for b in range(OBLK):
        out_ref[b] = total[b]

    spill = noted[0]
    for i in range(1, 32):
        spill = jnp.maximum(spill, noted[i])
    spill_ref[...] = spill

    for k in range(16):
        if RELAYED <= k < RELAYED + RELAYS:
            r = k - RELAYED
            sent(packed.at[k], relay_send.at[r])
            sent(relay.at[r, 0], forward_send.at[r, 0])
            sent(relay.at[r, pl.ds(1, 2)], forward_send.at[r, 1])
        else:
            sent(packed.at[k, 0], send_sem.at[k, 0])
            if k > 0:
                sent(packed.at[k, pl.ds(1, 2)], send_sem.at[k, 1])
        sent(got.at[k, 0, 1], cross_send.at[k])
        sent(back.at[k, 2], back_send.at[k, 1])
        if k > 0:
            sent(back.at[k, pl.ds(0, 2)], back_send.at[k, 0])

    def drain(j, carry):
        for i in range(3):
            sent(prod.at[j, i], z_send.at[j, i])
        sent(over.at[j], over_send.at[j])
        return carry

    lax.fori_loop(0, STEPS, drain, 0)
    sent(notes.at[pl.ds(1, 31)], note_send)


def spill_kernel(code0, code1, holds, amp_hbm, int_hbm, start_ref, out_ref,
                 amp, packed, got, bhi, blo, stage, lhs, prod, zgot, summed, back,
                 amp_sem, stage_sem, send_sem, got_sem, z_send, z_sem, back_send, back_sem):
    me = lax.axis_index("pair")
    z = lax.axis_index("red")
    x, y, c = me // 8, (me // 2) % 4, me % 2

    def device(off, core, sign=1):
        dx, dy = off
        if sign < 0:
            dx, dy = 4 - dx, 4 - dy
        return (lax.rem(x + dx, 4) * 4 + lax.rem(y + dy, 4)) * 2 + core

    def remote(src, dst, ssem, rsem, pair, layer):
        return pltpu.make_async_remote_copy(
            src_ref=src, dst_ref=dst, send_sem=ssem, recv_sem=rsem,
            device_id=(pair, layer), device_id_type=MESH)

    def received(dst, rsem):
        remote(dst, dst, send_sem.at[0], rsem, me + 1 - 2 * c, z).wait_recv()

    def sent(src, ssem):
        remote(src, src, ssem, got_sem.at[0], me + 1 - 2 * c, z).wait_send()

    barrier = pltpu.get_barrier_semaphore()

    def greet(i, carry):
        pl.semaphore_signal(barrier, inc=1, device_id=(2 * i + 1 - c, z), device_id_type=MESH)
        return carry

    lax.fori_loop(0, 16, greet, 0)
    for i in range(1, 4):
        pl.semaphore_signal(barrier, inc=1, device_id=(me, lax.rem(z + i, 4)), device_id_type=MESH)

    amp_copy = pltpu.make_async_copy(amp_hbm, amp, amp_sem)
    amp_copy.start()

    def load_stage(i):
        return pltpu.make_async_copy(int_hbm.at[0, pl.ds(i * 256, 256), :], stage.at[i % 2], stage_sem.at[i % 2])

    load_stage(0).start()
    load_stage(1).start()
    amp_copy.wait()

    def spilled(k):
        near, far = holds[device(OFFSETS[k], c)], holds[device(OFFSETS[k], 1 - c)]
        return code1[far], (code1[near] > code0[near]) & (code1[far] > code0[far])

    for k in range(16):
        code, used = spilled(k)
        packed[k] = amp[jnp.where(used, code, 0) // OBLK]
    pl.semaphore_wait(barrier, 19)
    for k in range(16):
        remote(packed.at[k], got.at[k], send_sem.at[k], got_sem.at[k], device(OFFSETS[k], 1 - c), z).start()

    for i in range(9):
        load_stage(i).wait()
        split_rows(stage.at[i % 2], bhi, blo, i * 256, z)
        if i + 2 < 9:
            load_stage(i + 2).start()

    def finish(j):
        for n in range(3):
            received(zgot.at[j, n], z_sem.at[j, n])
        for t in range(4):
            k, at = 4 * j + t, slice(t * 16, t * 16 + 16)
            summed[k] = (prod[j, 3, at, :] + zgot[j, 0, at, :]) + (zgot[j, 1, at, :] + zgot[j, 2, at, :])
            remote(summed.at[k], back.at[k], back_send.at[k], back_sem.at[k], device(OFFSETS[k], 1 - c, -1), z).start()

    for j in range(4):
        for t in range(4):
            k = 4 * j + t
            received(got.at[k], got_sem.at[k])
            part = got[k]
            high = part.astype(jnp.bfloat16)
            lhs[t * 16:t * 16 + 16, :] = high
            lhs[t * 16 + 64:t * 16 + 80, :] = (part - high.astype(jnp.float32)).astype(jnp.bfloat16)

        def columns(i, carry):
            both = jnp.dot(lhs[...], bhi[i], preferred_element_type=jnp.float32)
            low = jnp.dot(lhs[0:64, :], blo[i], preferred_element_type=jnp.float32)
            term = both[0:64] + (both[64:128] + low)
            prod[j, 2 * i] = term[:, 0:ZCOL]
            prod[j, 2 * i + 1] = term[:, ZCOL:2 * ZCOL]
            return carry

        lax.fori_loop(0, 2, columns, 0)
        for n in range(3):
            remote(prod.at[j, n], zgot.at[j, n], z_send.at[j, n], z_sem.at[j, n], me, lax.rem(z + 1 + n, 4)).start()
        if j:
            finish(j - 1)
    finish(3)

    out_ref[...] = start_ref[...]
    for k in range(16):
        code, used = spilled(k)
        received(back.at[k], back_sem.at[k])
        for b in range(OBLK):
            weight = jnp.where(used & (code % OBLK == b), 1.0, 0.0)
            out_ref[b] += weight * back[k]

    for k in range(16):
        sent(packed.at[k], send_sem.at[k])
        sent(summed.at[k], back_send.at[k])
    for j in range(4):
        for n in range(3):
            sent(prod.at[j, n], z_send.at[j, n])


def shards(amplitudes, tile_occ, tile_virt, owner, integrals):
    slots = amplitudes.shape[0]
    ids = jnp.arange(32, dtype=jnp.int32)
    code = jnp.arange(slots, dtype=jnp.int32) * OBLK + tile_occ
    names = tile_virt[:, 0][:, None] == ids[None, :]
    code0 = jnp.min(jnp.where(names, code[:, None], NONE), axis=0)
    code1 = jnp.max(jnp.where(names, code[:, None], -1), axis=0)
    holds = jnp.sum(jnp.where(owner[:, None] == ids[None, :], ids[:, None], 0), axis=0)
    f32, bf16 = jnp.float32, jnp.bfloat16
    dma = pltpu.SemaphoreType.DMA
    out, spill = pl.pallas_call(
        kernel,
        out_shape=(jax.ShapeDtypeStruct((OBLK, ROWS, ZCOL), f32), jax.ShapeDtypeStruct((8, 128), f32)),
        in_specs=[pl.BlockSpec(memory_space=pltpu.SMEM)] * 3 + [pl.BlockSpec(memory_space=pl.ANY)] * 2,
        out_specs=(pl.BlockSpec(memory_space=pltpu.VMEM),) * 2,
        scratch_shapes=[
            pltpu.VMEM((slots, ROWS, KDIM), f32),
            pltpu.VMEM((16, 3, ROWS, KDIM), f32),
            pltpu.VMEM((4, 3, ROWS, KDIM), f32),
            pltpu.VMEM((16, 2, 2, ROWS, KDIM), f32),
            pltpu.VMEM((2, KDIM, 2 * ZCOL), bf16),
            pltpu.VMEM((2, KDIM, 2 * ZCOL), bf16),
            pltpu.VMEM((2, 256, NCOL), f32),
            pltpu.VMEM((128, KDIM), bf16),
            pltpu.VMEM((STEPS, 4, 48, ZCOL), f32),
            pltpu.VMEM((STEPS, 3, 48, ZCOL), f32),
            pltpu.VMEM((STEPS, 3, ROWS, ZCOL), f32),
            pltpu.VMEM((16, 3, ROWS, ZCOL), f32),
            pltpu.VMEM((STEPS, ROWS, NCOL), f32),
            pltpu.VMEM((STEPS, ROWS, NCOL), f32),
            pltpu.VMEM((32, 8, 128), f32),
            pltpu.VMEM((32, 8, 128), f32),
            dma, dma((2,)), dma((16, 2)), dma((16, 3)), dma((4,)), dma((4,)), dma((4, 2)), dma((16,)),
            dma((STEPS, 3)), dma((STEPS, 3)), dma((16, 2)), dma((16, 2)), dma((STEPS,)), dma((STEPS,)), dma, dma,
        ],
        compiler_params=pltpu.CompilerParams(
            collective_id=0, has_side_effects=True, vmem_limit_bytes=64 * 2**20 - 2**17),
        cost_estimate=pl.CostEstimate(
            flops=6 * 1024 * KDIM * NCOL, bytes_accessed=4 * (KDIM * NCOL + slots * ROWS * KDIM), transcendentals=0),
    )(code0, code1, holds, amplitudes, integrals)

    def add_spilled(first):
        return pl.pallas_call(
            spill_kernel,
            out_shape=jax.ShapeDtypeStruct((OBLK, ROWS, ZCOL), f32),
            in_specs=[pl.BlockSpec(memory_space=pltpu.SMEM)] * 3 + [pl.BlockSpec(memory_space=pl.ANY)] * 2
            + [pl.BlockSpec(memory_space=pltpu.VMEM)],
            out_specs=pl.BlockSpec(memory_space=pltpu.VMEM),
            scratch_shapes=[
                pltpu.VMEM((slots, ROWS, KDIM), f32),
                pltpu.VMEM((16, ROWS, KDIM), f32),
                pltpu.VMEM((16, ROWS, KDIM), f32),
                pltpu.VMEM((2, KDIM, 2 * ZCOL), bf16),
                pltpu.VMEM((2, KDIM, 2 * ZCOL), bf16),
                pltpu.VMEM((2, 256, NCOL), f32),
                pltpu.VMEM((128, KDIM), bf16),
                pltpu.VMEM((4, 4, 64, ZCOL), f32),
                pltpu.VMEM((4, 3, 64, ZCOL), f32),
                pltpu.VMEM((16, ROWS, ZCOL), f32),
                pltpu.VMEM((16, ROWS, ZCOL), f32),
                dma, dma((2,)), dma((16,)), dma((16,)), dma((4, 3)), dma((4, 3)), dma((16,)), dma((16,)),
            ],
            compiler_params=pltpu.CompilerParams(
                collective_id=1, has_side_effects=True, vmem_limit_bytes=60 * 2**20),
            cost_estimate=pl.CostEstimate(
                flops=6 * 256 * KDIM * NCOL, bytes_accessed=4 * (KDIM * NCOL + slots * ROWS * KDIM), transcendentals=0),
        )(code0, code1, holds, amplitudes, integrals, first)

    return lax.cond(spill[7, 0] > 0.0, add_spilled, lambda first: first, out)


def solution(mesh):
    return jax.shard_map(
        shards,
        mesh=mesh,
        in_specs=(P("pair", None, "red"), P("pair"), P("pair", None), P(), P("pair", "red", None)),
        out_specs=P("pair", None, "red"),
        check_vma=False,
    )
```
